32 devices in a mesh: row: 8 (over z, y), col: 4 (over x, core).
Axes of the slice: x: 2, y: 2, z: 4, core: 2. Of those that a mesh axis runs over, the one named last changes fastest.
Arguments:
- a_blocks: float32 [128, 8, 125, 125], P('row', 'col'), may hold values from -0.1875 to 0.1875
- a_pattern: int32 [128, 8], P('row', 'col'), may hold values 0 or 1
- row_owner: int32 [128], replicated, may hold values from 0 to 127, as said below
- prolong: float32 [8, 24, 125, 125], P('row', 'col'), may hold values from -6 to 6
- p_pattern: int32 [8, 24], P('row', 'col'), may hold values 0 or 1
- prolong_slab: float32 [128, 8, 125, 125], P('row'), may hold values from -0.0625 to 0.0625
Outputs:
- coarse: float32 [8, 24, 125, 125], P('row', 'col')
The draws below stay inside these ranges and needn't reach their ends.
Inputs may be any that keep to these rules, and one draw needn't show every extreme that they name: row_owner is a permutation; the 16 element-order rows e with e // 16 equal go to at most 2 positions p of any one value p // 16, and exactly 2 for each value they reach.
All inputs are finite; a program needn't handle non-finite values. No bound on the sum of `a_pattern` or of `p_pattern` on one device may be relied on, other than what follows from the above.
Results may differ from the reference program's by a relative error of at most 0.0001.
Values sent between devices are 32-bit elements; how exact they have to be, the bound alone decides.
A program may use at most 128 MiB of HBM per device.

```python
import jax
import jax.numpy as jnp
from jax import lax

B = 125
MB = 16
CAP = 2
FINE = 128
K = 8
NC = 24
NA = 8
N_ROW = 8


def draw_row_owner(key, part):
    count = FINE // MB
    first_key, second_key = jax.random.split(key)
    sigma = jax.random.permutation(first_key, count)
    slot_order = jax.vmap(lambda k: jax.random.permutation(k, MB))(jax.random.split(second_key, count))
    element = jnp.arange(FINE, dtype=jnp.int32)
    source = element // MB
    within = element % MB
    group_idx = within // CAP
    target = sigma[(source + group_idx) % count]
    return (target * MB + slot_order[target, within]).astype(jnp.int32)


def plant(values, own_key, low, top_value):
    shape = values.shape
    index_at = [jax.random.randint(jax.random.fold_in(own_key, axis), (), 0, shape[axis]) for axis in range(len(shape))]
    values = values.at[tuple(index_at)].set(low)
    longest = shape.index(max(shape))
    index_at[longest] = (index_at[longest] + 1) % shape[longest]
    return values.at[tuple(index_at)].set(top_value)


def spiked(entries, rng, source, target, parts, factor):
    owner, partner = [(jnp.arange(entries.shape[axis_at]) // (entries.shape[axis_at] // parts)).reshape([-1 if axis == axis_at else 1 for axis in range(entries.ndim)]) for axis_at in (source, target)]
    chosen = jax.random.permutation(rng, parts)[partner]
    strong = (owner == chosen) | (owner == (partner + parts // 2) % parts)
    return jnp.where(strong, factor * entries, entries)


def block_scale(stream_key, shape, cuts, smallest, top_value):
    def one(axis_at, parts):
        heights = jax.random.uniform(jax.random.fold_in(jax.random.fold_in(stream_key, 6), axis_at), (parts,), jnp.float32, smallest / len(cuts), top_value / len(cuts))
        return jnp.repeat(jnp.exp(heights), shape[axis_at] // parts).reshape((-1,) + (1,) * (len(shape) - axis_at - 1))

    level = one(*cuts[0])
    for cut in cuts[1:]:
        level = level * one(*cut)
    return level


def gaussian(rng, shape, width, most, cuts=(), kind=jnp.bfloat16):
    array = jax.random.normal(rng, shape, jnp.float32) * width
    if len(cuts) > 0:
        array = block_scale(rng, shape, cuts, -0.22, 0.18) * array
    return jnp.clip(array, min=-most, max=most).astype(kind)


def gaussian_with(stream_key, shape, width, reach, cuts, heavy, kind=jnp.bfloat16):
    entries = width * jax.random.normal(stream_key, shape, jnp.float32)
    if cuts:
        entries = entries * block_scale(stream_key, shape, cuts, -0.22, 0.18)
    return jnp.clip(spiked(entries, jax.random.fold_in(stream_key, 3), *heavy), -reach, reach).astype(kind)


def setup_inputs(seed: int = 0) -> dict:
    seeds = jax.random.split(jax.random.key(seed), 7)
    return {
        "a_blocks": gaussian(seeds[0], (FINE, K, B, B), (B * K) ** -0.5, 0.1875, ((0, 8), (1, 4)), jnp.float32),
        "a_pattern": plant((jax.random.randint(seeds[1], (FINE, K), 0, 2) < 1).astype(jnp.int32), jax.random.fold_in(seeds[1], 1), 0, 1),
        "row_owner": draw_row_owner(jax.random.fold_in(seeds[6], 71), 0),
        "prolong": gaussian(seeds[3], (K, NC, B, B), 1.0, 6.0, ((0, 8), (1, 4)), jnp.float32),
        "p_pattern": plant((jax.random.randint(seeds[4], (K, NC), 0, 2) < 1).astype(jnp.int32), jax.random.fold_in(seeds[4], 1), 0, 1),
        "prolong_slab": gaussian_with(seeds[5], (FINE, NA, B, B), (B * FINE) ** -0.5, 0.0625, ((0, 8),), (0, 1, 8, 2.0), jnp.float32),
    }


def reference(a_blocks, a_pattern, row_owner, prolong, p_pattern, prolong_slab):
    masked = a_blocks * a_pattern.astype(a_blocks.dtype)[:, :, None, None]
    grid_a = jnp.zeros_like(masked).at[row_owner.astype(jnp.int32)].set(masked)
    p_masked = prolong * p_pattern.astype(prolong.dtype)[:, :, None, None]
    grouped_a = grid_a.reshape((N_ROW, MB) + grid_a.shape[1:])
    grouped_slab = prolong_slab.reshape((N_ROW, MB) + prolong_slab.shape[1:])

    def one_group(total, pieces):
        rows_a, rows_slab = pieces
        product = jnp.einsum("mkxy,knyz->mnxz", rows_a, p_masked, precision=lax.Precision.HIGHEST)
        return total + jnp.einsum("maxy,mnxz->anyz", rows_slab, product, precision=lax.Precision.HIGHEST), None

    start = jnp.zeros((NA, NC, B, B), dtype=a_blocks.dtype)
    coarse, _ = lax.scan(one_group, start, (grouped_a, grouped_slab))
    return coarse
```

```python
import functools

import jax
import jax.numpy as jnp
from jax import lax
from jax.experimental import pallas as pl
from jax.experimental.pallas import tpu as pltpu
from jax.sharding import PartitionSpec as P

CAP = 2
Z = 4
L = 128
WAVES = 4
PARTS = 2
MESH = pl.DeviceIdType.MESH
VMEM_LIMIT = 58 * 1024 * 1024

P_NEAR = (0, 3)
P_FAR = ((0, 0), (0, 0))
P_IN = ((2, 1), (2, 3))
P_OUT = ((2, 5), (3, 1))


def split(v):
    hi = v.astype(jnp.bfloat16)
    lo = (v - hi.astype(jnp.float32)).astype(jnp.bfloat16)
    return hi, lo


def dot(a, b):
    return jnp.dot(a, b, preferred_element_type=jnp.float32)


def kernel(
    R, C, KEEP, a_hbm, s_hbm, p_in, owner, a_pat, p_pat, out,
    a_v, s_v, flip, asend, arecv, stage, sh, sl, ahl, macc, yrecv, nbuf, frecv, nrecv, crecv,
    mfull, mth, mtl, pbuf, ph, plo, total,
    load, a_s, a_r, y_s, y_r, f_s, f_r, n_s, n_r, c_s, c_r, g_s, g_r, pn_s, pf_s, pw_s, py_s, p_r,
):
    KP, W, B = a_pat.shape[0], a_pat.shape[1], a_v.shape[1]
    NA, NJ = s_v.shape[1] // B, p_in.shape[0]
    NV, RV = WAVES, KP * L // WAVES
    H, Q = L // RV, NJ // PARTS
    Y = R // Z
    f32 = jnp.float32
    me, col = lax.axis_index("row"), lax.axis_index("col")
    z, y = lax.div(me, Y), lax.rem(me, Y)
    near0 = 2 * lax.div(z, 2)
    far0 = 2 - near0
    zn = 2 * near0 + 1 - z
    inner = (z == 1) | (z == 2)
    far_inner = jnp.where(z < 2, 2, 1)

    load_a = pltpu.make_async_copy(a_hbm, a_v, load.at[0])
    load_s = pltpu.make_async_copy(s_hbm, s_v, load.at[1])
    load_a.start()
    load_s.start()

    barrier = pltpu.get_barrier_semaphore()
    for i in range(1, R):
        pl.semaphore_signal(barrier, inc=1, device_id={"row": lax.rem(me + i, R)}, device_id_type=MESH)
    for i in range(1, C):
        pl.semaphore_signal(barrier, inc=1, device_id={"col": lax.rem(col + i, C)}, device_id_type=MESH)

    def pair(source, target):
        first, last = jnp.int32(W), jnp.int32(-1)
        for e in range(W):
            hit = lax.div(owner[source * W + e], W) == target
            first = jnp.minimum(first, jnp.where(hit, e, W))
            last = jnp.maximum(last, jnp.where(hit, e, -1))
        valid = last >= 0
        return (jnp.where(valid, first, 0), jnp.where(valid, last, 0)), valid

    def step_of(j):
        half = lax.div(j + 1, 2)
        return R // 2 + half * (1 - 2 * lax.rem(j, 2))

    def a_copy(v, step):
        return pltpu.make_async_remote_copy(
            src_ref=asend.at[v, step], dst_ref=arecv.at[v, step], send_sem=a_s.at[v, step], recv_sem=a_r.at[v, step],
            device_id={"row": lax.rem(me + step, R)}, device_id_type=MESH,
        )

    def pack(buf, step, k):
        rows, valid = pair(me, lax.rem(me + step, R))
        for s in range(CAP):
            scale = jnp.where(valid, a_pat[k, rows[s]], 0).astype(f32)
            flip[s, 0:B, 0:B] = a_v[pl.ds(rows[s] * (B * KP) + k, B, stride=KP), :] * scale
        for s in range(CAP):
            turned = flip[s].T
            for h in range(H):
                buf[k * H + h, step, s] = turned[h * RV : (h + 1) * RV]

    def p_copy(slot, q, target, s_sem):
        at = pl.ds(q * Q, Q)
        return pltpu.make_async_remote_copy(
            src_ref=pbuf.at[slot, at], dst_ref=pbuf.at[slot, at], send_sem=s_sem, recv_sem=p_r.at[slot, q],
            device_id={"row": target}, device_id_type=MESH,
        )

    def p_near(q):
        return p_copy(me, q, zn * Y + y, pn_s.at[q])

    def p_far(q):
        return p_copy(me, q, far_inner * Y + y, pf_s.at[q])

    def p_forward(u, q):
        return p_copy((far0 + u) * Y + y, q, zn * Y + y, pw_s.at[u, q])

    def p_across(zo, i, q):
        return p_copy(zo * Y + y, q, z * Y + lax.rem(y + i, Y), py_s.at[zo, i, q])

    def p_arrived(slot, q):
        p_copy(slot, q, me, pn_s.at[q]).wait_recv()

    def all_across(zo, q):
        for i in range(1, Y):
            p_across(zo, i, q).start()

    def near_arrives(q):
        p_arrived(zn * Y + y, q)
        all_across(zn, q)

    def far_arrives(q):
        for u in range(2):
            p_arrived((far0 + u) * Y + y, q)

            @pl.when(inner)
            def _():
                p_forward(u, q).start()

            all_across(far0 + u, q)

    def y_copy(v, i, h):
        target = lax.rem(y + i, Y)
        at = pl.ds(near0 if h else far0, 2)
        return pltpu.make_async_remote_copy(
            src_ref=macc.at[v, target, at], dst_ref=yrecv.at[v, i, at], send_sem=y_s.at[v, i, h], recv_sem=y_r.at[v, i, h],
            device_id={"row": z * Y + target}, device_id_type=MESH,
        )

    def f_copy(v):
        return pltpu.make_async_remote_copy(
            src_ref=nbuf.at[v, pl.ds(far0, 2)], dst_ref=frecv.at[v], send_sem=f_s.at[v], recv_sem=f_r.at[v],
            device_id={"row": zn * Y + y}, device_id_type=MESH,
        )

    def n_copy(v):
        return pltpu.make_async_remote_copy(
            src_ref=nbuf.at[v, zn], dst_ref=nrecv.at[v], send_sem=n_s.at[v], recv_sem=n_r.at[v],
            device_id={"row": zn * Y + y}, device_id_type=MESH,
        )

    def c_copy(v, u):
        return pltpu.make_async_remote_copy(
            src_ref=nbuf.at[v, far0 + u], dst_ref=crecv.at[v], send_sem=c_s.at[v, u], recv_sem=c_r.at[v],
            device_id={"row": (far0 + u) * Y + y}, device_id_type=MESH,
        )

    def g_copy(v, i):
        at = pl.ds(pl.multiple_of(col * RV, RV), RV)
        return pltpu.make_async_remote_copy(
            src_ref=mfull.at[v, at], dst_ref=mfull.at[v, at], send_sem=g_s.at[v, i], recv_sem=g_r.at[v, i],
            device_id={"col": lax.rem(col + i, C)}, device_id_type=MESH,
        )

    def over_y(v):
        for h in range(2):
            for i in range(1, Y):
                y_copy(v, i, h).start()

    def over_near(v):
        for h in range(2):
            at = pl.ds(near0 if h else far0, 2)
            acc = macc[v, y, at]
            for i in range(1, Y):
                y_copy(v, i, h).wait_recv()
                acc += yrecv[v, i, at]
            nbuf[v, at] = acc
            if h == 0:
                @pl.when(jnp.logical_not(inner))
                def _():
                    f_copy(v).start()
            else:
                n_copy(v).start()

    def over_middle(v):
        @pl.when(inner)
        def _():
            f_copy(v).wait_recv()
            nbuf[v, pl.ds(far0, 2)] += frecv[v]
            for u in range(2):
                c_copy(v, u).start()

    def over_col(v):
        n_copy(v).wait_recv()
        c_copy(v, 0).wait_recv()
        mfull[v, pl.ds(pl.multiple_of(col * RV, RV), RV)] = nbuf[v, z] + nrecv[v] + crecv[v]
        for i in range(1, C):
            g_copy(v, i).start()

    def last_product(v):
        for i in range(1, C):
            g_copy(v, i).wait_recv()
        for c in range(C * RV // L):
            hi, lo = split(mfull[v, c * L : (c + 1) * L].T)
            mth[:, c * L : (c + 1) * L] = hi
            mtl[:, c * L : (c + 1) * L] = lo
        total[...] += dot(mth[...], ph[v]) + (dot(mth[...], plo[v]) + dot(mtl[...], ph[v]))

    flip[...] = jnp.zeros_like(flip)
    load_a.wait()

    def first_pack(j, carry):
        pack(asend, step_of(j), 0)
        return carry

    lax.fori_loop(0, R - 1, first_pack, 0)
    pl.semaphore_wait(barrier, R + C - 2)

    for v in range(H):
        def send(j, carry):
            a_copy(v, step_of(j)).start()
            return carry

        lax.fori_loop(0, R - 1, send, 0)

    for k in range(1, KP):
        def pack_send(j, carry):
            step = step_of(j)
            pack(asend, step, k)
            a_copy(k * H, step).start()
            return carry

        lax.fori_loop(0, R - 1, pack_send, 0)
        for h in range(1, H):
            def send_rest(j, carry):
                a_copy(k * H + h, step_of(j)).start()
                return carry

            lax.fori_loop(0, R - 1, send_rest, 0)

    for n in range(NJ):
        pbuf[me, n] = jnp.zeros((L, L), f32)
        pbuf[me, n, 0:B, 0:B] = p_in[n, :, 0, :] * p_pat[0, n].astype(f32)
    for q in range(PARTS):
        p_near(q).start()
        all_across(z, q)
    for k in range(KP):
        pack(arecv, 0, k)
    stage[...] = jnp.zeros_like(stage)
    macc[...] = jnp.zeros_like(macc)
    total[...] = jnp.zeros_like(total)
    load_s.wait()

    def slab(step, keep):
        source = lax.rem(me - step + R, R)
        rows, valid = pair(source, me)
        for s in range(CAP):
            g = jnp.where(valid, owner[source * W + rows[s]] - me * W, 0)

            def one(b, carry):
                for h in range(2):
                    stage[2 * b + h, 0:B, 0:B] = s_v[g, pl.ds(2 * b + h, B, stride=NA), :]
                for h in range(2):
                    hi, lo = split(stage[2 * b + h])
                    sh[keep, b, s * L : (s + 1) * L, h * L : (h + 1) * L] = hi
                    sl[keep, b, s * L : (s + 1) * L, h * L : (h + 1) * L] = lo
                return carry

            lax.fori_loop(0, NA // 2, one, 0)

    def work(t, carry):
        v, j = lax.div(t, R), lax.rem(t, R)
        step = jnp.where(j == 0, 0, step_of(j - 1))
        keep = step if KEEP else 0
        if KEEP:
            @pl.when(v == 0)
            def _():
                slab(step, step)
        else:
            slab(step, 0)

        @pl.when(j > 0)
        def _():
            a_copy(v, step).wait_recv()

        for s in range(CAP):
            hi, lo = split(arecv[v, step, s])
            ahl[0:RV, s * L : (s + 1) * L] = hi
            ahl[RV : 2 * RV, s * L : (s + 1) * L] = lo
        for b in range(NA // 2):
            both = dot(ahl[...], sh[keep, b])
            r = both[0:RV] + (both[RV : 2 * RV] + dot(ahl[0:RV], sl[keep, b]))
            for h in range(2):
                a = 2 * b + h
                macc[v, a % Y, a // Y] += r[:, h * L : (h + 1) * L]

        def at(when, act):
            @pl.when((v == when[0]) & (j == when[1]))
            def _():
                act()

        def chain(when, act):
            @pl.when((v > 0) & (j == when))
            def _():
                act(v - 1)

        @pl.when(j == R - 1)
        def _():
            over_y(v)

        chain(R // 2 - 2, over_near)
        chain(R // 2, over_middle)
        chain(R // 2 + 2, over_col)
        for q in range(PARTS):
            at(P_FAR[q], lambda q=q: p_far(q).start())
            at(P_NEAR, lambda q=q: near_arrives(q))

            @pl.when(inner)
            def _():
                at(P_IN[q], lambda q=q: far_arrives(q))

            @pl.when(jnp.logical_not(inner))
            def _():
                at(P_OUT[q], lambda q=q: far_arrives(q))
        return carry

    lax.fori_loop(0, NV * R, work, 0)

    for q in range(PARTS):
        for zo in range(Z):
            for i in range(1, Y):
                p_arrived(zo * Y + lax.rem(y + i, Y), q)

    def p_split(r, carry):
        c, k = lax.div(r, KP), lax.rem(r, KP)
        at = pl.ds(pl.multiple_of(c * RV, RV), RV)
        for n in range(NJ):
            hi, lo = split(pbuf[r, n])
            for h in range(H):
                ph[k * H + h, at, n * L : (n + 1) * L] = hi[h * RV : (h + 1) * RV]
                plo[k * H + h, at, n * L : (n + 1) * L] = lo[h * RV : (h + 1) * RV]
        return carry

    lax.fori_loop(0, R, p_split, 0)
    for v in range(NV - 1):
        last_product(v)
    over_near(NV - 1)
    over_middle(NV - 1)
    over_col(NV - 1)
    last_product(NV - 1)

    for n in range(NJ):
        out[0, n] = total[0:B, n * L : n * L + B]

    def sent(v, carry):
        def one(j, carry):
            a_copy(v, j + 1).wait_send()
            return carry

        lax.fori_loop(0, R - 1, one, 0)
        for i in range(1, Y):
            for h in range(2):
                y_copy(v, i, h).wait_send()
        n_copy(v).wait_send()

        @pl.when(inner)
        def _():
            for u in range(2):
                c_copy(v, u).wait_send()

        @pl.when(jnp.logical_not(inner))
        def _():
            f_copy(v).wait_send()

        for i in range(1, C):
            g_copy(v, i).wait_send()
        return carry

    lax.fori_loop(0, NV, sent, 0)
    for q in range(PARTS):
        p_near(q).wait_send()
        p_far(q).wait_send()

        @pl.when(inner)
        def _():
            for u in range(2):
                p_forward(u, q).wait_send()

        for zo in range(Z):
            for i in range(1, Y):
                p_across(zo, i, q).wait_send()


def shards(a_blocks, a_pattern, row_owner, prolong, p_pattern, prolong_slab):
    R, C = lax.axis_size("row"), lax.axis_size("col")
    W, KP, B = a_blocks.shape[:3]
    NA, NJ = prolong_slab.shape[1], prolong.shape[1]
    f32, bf16 = jnp.float32, jnp.bfloat16
    Y, NV, RV = R // Z, WAVES, KP * L // WAVES
    keep = R * NA <= 64
    slots = R if keep else 1
    oper = a_blocks.transpose(0, 2, 1, 3).reshape(W * B * KP, B)
    slab = prolong_slab.transpose(0, 2, 1, 3).reshape(W, B * NA, B)
    dma = pltpu.SemaphoreType.DMA
    vmem = pl.BlockSpec(memory_space=pltpu.VMEM)
    smem = pl.BlockSpec(memory_space=pltpu.SMEM)
    hbm = pl.BlockSpec(memory_space=pl.ANY)
    return pl.pallas_call(
        functools.partial(kernel, R, C, keep),
        out_shape=jax.ShapeDtypeStruct((1, NJ, B, B), f32),
        in_specs=[hbm, hbm, vmem, smem, smem, smem],
        out_specs=vmem,
        scratch_shapes=[
            pltpu.VMEM((W * B * KP, B), f32),
            pltpu.VMEM((W, B * NA, B), f32),
            pltpu.VMEM((CAP, L, L), f32),
            pltpu.VMEM((NV, R, CAP, RV, L), f32),
            pltpu.VMEM((NV, R, CAP, RV, L), f32),
            pltpu.VMEM((NA, L, L), f32),
            pltpu.VMEM((slots, NA // 2, CAP * L, 2 * L), bf16),
            pltpu.VMEM((slots, NA // 2, CAP * L, 2 * L), bf16),
            pltpu.VMEM((2 * RV, CAP * L), bf16),
            pltpu.VMEM((NV, Y, Z, RV, L), f32),
            pltpu.VMEM((NV, Y, Z, RV, L), f32),
            pltpu.VMEM((NV, Z, RV, L), f32),
            pltpu.VMEM((NV, 2, RV, L), f32),
            pltpu.VMEM((NV, RV, L), f32),
            pltpu.VMEM((NV, RV, L), f32),
            pltpu.VMEM((NV, C * RV, L), f32),
            pltpu.VMEM((L, C * RV), bf16),
            pltpu.VMEM((L, C * RV), bf16),
            pltpu.VMEM((R, NJ, L, L), f32),
            pltpu.VMEM((NV, C * RV, NJ * L), bf16),
            pltpu.VMEM((NV, C * RV, NJ * L), bf16),
            pltpu.VMEM((L, NJ * L), f32),
            dma((2,)),
            dma((NV, R)), dma((NV, R)),
            dma((NV, Y, 2)), dma((NV, Y, 2)),
            dma((NV,)), dma((NV,)), dma((NV,)), dma((NV,)),
            dma((NV, 2)), dma((NV,)),
            dma((NV, C)), dma((NV, C)),
            dma((PARTS,)), dma((PARTS,)), dma((2, PARTS)), dma((Z, Y, PARTS)), dma((R, PARTS)),
        ],
        compiler_params=pltpu.CompilerParams(
            collective_id=0, has_side_effects=True, vmem_limit_bytes=VMEM_LIMIT
        ),
    )(oper, slab, prolong.transpose(1, 2, 0, 3), row_owner, a_pattern.T, p_pattern)


def solution(mesh):
    in_specs = (
        P("row", "col", None, None),
        P("row", "col"),
        P(),
        P("row", "col", None, None),
        P("row", "col"),
        P("row", None, None, None),
    )
    out_specs = P("row", "col", None, None)
    return jax.shard_map(shards, mesh=mesh, in_specs=in_specs, out_specs=out_specs, check_vma=False)
```

```python
import functools

import jax
import jax.numpy as jnp
from jax import lax
from jax.experimental import pallas as pl
from jax.experimental.pallas import tpu as pltpu
from jax.sharding import PartitionSpec as P

CAP = 2
Z = 4
L = 128
WAVES = 4
PARTS = 3
WINDOW = 0.25
DIRECT = 1
MESH = pl.DeviceIdType.MESH
VMEM_LIMIT = 58 * 1024 * 1024

SUMS = (0.2, 0.4, 0.6)
OWN = 0.02
NEAR = 0.3
FAR = (0.25, 0.75)
INTO = 0.31
ONWARD = 0.12


def split(v):
    hi = v.astype(jnp.bfloat16)
    lo = (v - hi.astype(jnp.float32)).astype(jnp.bfloat16)
    return hi, lo


def dot(a, b):
    return jnp.dot(a, b, preferred_element_type=jnp.float32)


def kernel(
    R, C, KEEP, a_hbm, s_hbm, p_in, owner, a_pat, p_pat, out,
    a_v, s_v, flip, asend, arecv, stage, sh, sl, ahl, macc, yrecv, nbuf, frecv, nrecv, crecv, mrecv,
    mfull, mth, mtl, pbuf, ph, plo, total,
    load, a_s, a_r, y_s, y_r, f_s, f_r, n_s, n_r, c_s, c_r, m_s, m_r, g_s, g_r, pn_s, pf_s, pw_s, py_s, p_r,
):
    KP, W, B = a_pat.shape[0], a_pat.shape[1], a_v.shape[1]
    NA, NJ = s_v.shape[1] // B, p_in.shape[0]
    NV, RV = WAVES, KP * L // WAVES
    H, Q = L // RV, NJ // PARTS
    Y = R // Z
    f32 = jnp.float32
    me, col = lax.axis_index("row"), lax.axis_index("col")
    z, y = lax.div(me, Y), lax.rem(me, Y)
    near0 = 2 * lax.div(z, 2)
    far0 = 2 - near0
    zn = 2 * near0 + 1 - z
    inner = (z == 1) | (z == 2)
    far_inner = jnp.where(z < 2, 2, 1)

    load_a = pltpu.make_async_copy(a_hbm, a_v, load.at[0])
    load_s = pltpu.make_async_copy(s_hbm, s_v, load.at[1])
    load_a.start()
    load_s.start()

    barrier = pltpu.get_barrier_semaphore()
    for i in range(1, R):
        pl.semaphore_signal(barrier, inc=1, device_id={"row": lax.rem(me + i, R)}, device_id_type=MESH)
    for i in range(1, C):
        pl.semaphore_signal(barrier, inc=1, device_id={"col": lax.rem(col + i, C)}, device_id_type=MESH)

    def pair(source, target):
        first, last = jnp.int32(W), jnp.int32(-1)
        for e in range(W):
            hit = lax.div(owner[source * W + e], W) == target
            first = jnp.minimum(first, jnp.where(hit, e, W))
            last = jnp.maximum(last, jnp.where(hit, e, -1))
        valid = last >= 0
        return (jnp.where(valid, first, 0), jnp.where(valid, last, 0)), valid

    def step_of(j):
        half = lax.div(j + 1, 2)
        return R // 2 + half * (1 - 2 * lax.rem(j, 2))

    def a_copy(v, step):
        return pltpu.make_async_remote_copy(
            src_ref=asend.at[v, step], dst_ref=arecv.at[v, step], send_sem=a_s.at[v, step], recv_sem=a_r.at[v, step],
            device_id={"row": lax.rem(me + step, R)}, device_id_type=MESH,
        )

    def pack(buf, step, k):
        rows, valid = pair(me, lax.rem(me + step, R))
        for s in range(CAP):
            scale = jnp.where(valid, a_pat[k, rows[s]], 0).astype(f32)
            flip[s, 0:B, 0:B] = a_v[pl.ds(rows[s] * (B * KP) + k, B, stride=KP), :] * scale
        for s in range(CAP):
            turned = flip[s].T
            for h in range(H):
                buf[k * H + h, step, s] = turned[h * RV : (h + 1) * RV]

    def p_copy(slot, q, target, s_sem):
        at = pl.ds(q * Q, Q)
        return pltpu.make_async_remote_copy(
            src_ref=pbuf.at[slot, at], dst_ref=pbuf.at[slot, at], send_sem=s_sem, recv_sem=p_r.at[slot, q],
            device_id={"row": target}, device_id_type=MESH,
        )

    def p_near(q):
        return p_copy(me, q, zn * Y + y, pn_s.at[q])

    def p_far(q):
        return p_copy(me, q, far_inner * Y + y, pf_s.at[q])

    def p_forward(u, q):
        return p_copy((far0 + u) * Y + y, q, zn * Y + y, pw_s.at[u, q])

    def p_across(zo, i, q):
        return p_copy(zo * Y + y, q, z * Y + lax.rem(y + i, Y), py_s.at[zo, i, q])

    def p_arrived(slot, q):
        p_copy(slot, q, me, pn_s.at[q]).wait_recv()

    def all_across(zo, q):
        for i in range(1, Y):
            p_across(zo, i, q).start()

    def near_arrives(q):
        p_arrived(zn * Y + y, q)
        all_across(zn, q)

    def far_arrives(q):
        for u in range(2):
            p_arrived((far0 + u) * Y + y, q)

            @pl.when(inner)
            def _():
                p_forward(u, q).start()

            all_across(far0 + u, q)

    def y_copy(v, i, h):
        target = lax.rem(y + i, Y)
        at = pl.ds(near0 if h else far0, 2)
        return pltpu.make_async_remote_copy(
            src_ref=macc.at[v, target, at], dst_ref=yrecv.at[v, i, at], send_sem=y_s.at[v, i, h], recv_sem=y_r.at[v, i, h],
            device_id={"row": z * Y + target}, device_id_type=MESH,
        )

    def f_copy(v):
        return pltpu.make_async_remote_copy(
            src_ref=nbuf.at[v, pl.ds(far0, 2)], dst_ref=frecv.at[v], send_sem=f_s.at[v], recv_sem=f_r.at[v],
            device_id={"row": zn * Y + y}, device_id_type=MESH,
        )

    def n_copy(v):
        return pltpu.make_async_remote_copy(
            src_ref=nbuf.at[v, zn], dst_ref=nrecv.at[v], send_sem=n_s.at[v], recv_sem=n_r.at[v],
            device_id={"row": zn * Y + y}, device_id_type=MESH,
        )

    def c_copy(v, u):
        return pltpu.make_async_remote_copy(
            src_ref=nbuf.at[v, far0 + u], dst_ref=crecv.at[v], send_sem=c_s.at[v, u], recv_sem=c_r.at[v],
            device_id={"row": (far0 + u) * Y + y}, device_id_type=MESH,
        )

    def g_copy(v, i):
        at = pl.ds(pl.multiple_of(col * RV, RV), RV)
        return pltpu.make_async_remote_copy(
            src_ref=mfull.at[v, at], dst_ref=mfull.at[v, at], send_sem=g_s.at[v, i], recv_sem=g_r.at[v, i],
            device_id={"col": lax.rem(col + i, C)}, device_id_type=MESH,
        )

    def over_y(v):
        for h in range(2):
            for i in range(1, Y):
                y_copy(v, i, h).start()

    def over_near(v):
        for h in range(2):
            at = pl.ds(near0 if h else far0, 2)
            acc = macc[v, y, at]
            for i in range(1, Y):
                y_copy(v, i, h).wait_recv()
                acc += yrecv[v, i, at]
            nbuf[v, at] = acc
            if h == 0:
                @pl.when(jnp.logical_not(inner))
                def _():
                    f_copy(v).start()
            else:
                n_copy(v).start()

    def over_middle(v):
        @pl.when(inner)
        def _():
            f_copy(v).wait_recv()
            nbuf[v, pl.ds(far0, 2)] += frecv[v]
            for u in range(2):
                c_copy(v, u).start()

    def over_col(v):
        n_copy(v).wait_recv()
        c_copy(v, 0).wait_recv()
        mfull[v, pl.ds(pl.multiple_of(col * RV, RV), RV)] = nbuf[v, z] + nrecv[v] + crecv[v]
        for i in range(1, C):
            g_copy(v, i).start()

    def m_copy(v, step):
        target = lax.rem(me + step, R)
        d = jnp.maximum(v - (NV - DIRECT), 0)
        return pltpu.make_async_remote_copy(
            src_ref=macc.at[v, lax.rem(target, Y), lax.div(target, Y)], dst_ref=mrecv.at[d, step],
            send_sem=m_s.at[d, step], recv_sem=m_r.at[d, step],
            device_id={"row": target}, device_id_type=MESH,
        )

    def over_rows(v):
        def one(j, carry):
            m_copy(v, step_of(j)).start()
            return carry

        lax.fori_loop(0, R - 1, one, 0)

    def col_after_rows(v):
        acc = macc[v, y, z]
        for step in range(1, R):
            m_copy(v, step).wait_recv()
            acc += mrecv[v - (NV - DIRECT), step]
        mfull[v, pl.ds(pl.multiple_of(col * RV, RV), RV)] = acc
        for i in range(1, C):
            g_copy(v, i).start()

    def last_product(v):
        for i in range(1, C):
            g_copy(v, i).wait_recv()
        for c in range(C * RV // L):
            hi, lo = split(mfull[v, c * L : (c + 1) * L].T)
            mth[:, c * L : (c + 1) * L] = hi
            mtl[:, c * L : (c + 1) * L] = lo
        total[...] += dot(mth[...], ph[v]) + (dot(mth[...], plo[v]) + dot(mtl[...], ph[v]))

    flip[...] = jnp.zeros_like(flip)
    load_a.wait()

    def first_pack(j, carry):
        pack(asend, step_of(j), 0)
        return carry

    lax.fori_loop(0, R - 1, first_pack, 0)
    pl.semaphore_wait(barrier, R + C - 2)

    def send(n, carry):
        a_copy(lax.div(n, R - 1), step_of(lax.rem(n, R - 1))).start()
        return carry

    window = min(int(WINDOW * NV * R), H * (R - 1))
    lax.fori_loop(0, window, send, 0)

    for k in range(1, KP):
        def later_pack(j, carry):
            pack(asend, step_of(j), k)
            return carry

        lax.fori_loop(0, R - 1, later_pack, 0)

    for n in range(NJ):
        pbuf[me, n] = jnp.zeros((L, L), f32)
        pbuf[me, n, 0:B, 0:B] = p_in[n, :, 0, :] * p_pat[0, n].astype(f32)
    for k in range(KP):
        pack(arecv, 0, k)
    stage[...] = jnp.zeros_like(stage)
    macc[...] = jnp.zeros_like(macc)
    total[...] = jnp.zeros_like(total)
    load_s.wait()

    def slab(step, keep):
        source = lax.rem(me - step + R, R)
        rows, valid = pair(source, me)
        for s in range(CAP):
            g = jnp.where(valid, owner[source * W + rows[s]] - me * W, 0)

            def one(b, carry):
                for h in range(2):
                    stage[2 * b + h, 0:B, 0:B] = s_v[g, pl.ds(2 * b + h, B, stride=NA), :]
                for h in range(2):
                    hi, lo = split(stage[2 * b + h])
                    sh[keep, b, s * L : (s + 1) * L, h * L : (h + 1) * L] = hi
                    sl[keep, b, s * L : (s + 1) * L, h * L : (h + 1) * L] = lo
                return carry

            lax.fori_loop(0, NA // 2, one, 0)

    def work(t, carry):
        v, j = lax.div(t, R), lax.rem(t, R)
        step = jnp.where(j == 0, 0, step_of(j - 1))
        keep = step if KEEP else 0
        if KEEP:
            @pl.when(v == 0)
            def _():
                slab(step, step)
        else:
            slab(step, 0)

        @pl.when(j > 0)
        def _():
            a_copy(v, step).wait_recv()
            ahead = v * (R - 1) + j - 1 + window

            @pl.when(ahead < NV * (R - 1))
            def _():
                send(ahead, 0)

        for s in range(CAP):
            hi, lo = split(arecv[v, step, s])
            ahl[0:RV, s * L : (s + 1) * L] = hi
            ahl[RV : 2 * RV, s * L : (s + 1) * L] = lo
        for b in range(NA // 2):
            both = dot(ahl[...], sh[keep, b])
            r = both[0:RV] + (both[RV : 2 * RV] + dot(ahl[0:RV], sl[keep, b]))
            for h in range(2):
                a = 2 * b + h
                macc[v, a % Y, a // Y] += r[:, h * L : (h + 1) * L]

        @pl.when((j == R - 1) & (v < NV - DIRECT))
        def _():
            over_y(v)

        @pl.when((j == R - 1) & (v >= NV - DIRECT))
        def _():
            over_rows(v)

        for when, act in todo:
            if when < NV * R:
                pl.when(t == when)(act)
        return carry

    def own_starts():
        for q in range(PARTS):
            p_near(q).start()
            all_across(z, q)

    def near_comes():
        for q in range(PARTS):
            near_arrives(q)

    def place(when):
        return int(when * NV * R)

    todo = [(place(OWN), own_starts), (place(NEAR), near_comes)]
    for q in range(PARTS):
        far = FAR[0] + (FAR[1] - FAR[0]) * q / max(PARTS - 1, 1)
        todo.append((place(far), lambda q=q: p_far(q).start()))
        todo.append((place(far + INTO), lambda q=q: pl.when(inner)(lambda: far_arrives(q))))
        todo.append((place(far + INTO + ONWARD), lambda q=q: pl.when(jnp.logical_not(inner))(lambda: far_arrives(q))))
    for v in range(NV - DIRECT):
        for d, act in enumerate((over_near, over_middle, over_col)):
            todo.append(((v + 1) * R - 1 + place(SUMS[d]), lambda v=v, act=act: act(v)))
    todo.sort(key=lambda item: item[0])

    lax.fori_loop(0, NV * R, work, 0)
    for when, act in todo:
        if when >= NV * R:
            act()
    for v in range(NV - DIRECT, NV):
        col_after_rows(v)

    for q in range(PARTS):
        for zo in range(Z):
            for i in range(1, Y):
                p_arrived(zo * Y + lax.rem(y + i, Y), q)

    def p_split(r, carry):
        c, k = lax.div(r, KP), lax.rem(r, KP)
        at = pl.ds(pl.multiple_of(c * RV, RV), RV)
        for n in range(NJ):
            hi, lo = split(pbuf[r, n])
            for h in range(H):
                ph[k * H + h, at, n * L : (n + 1) * L] = hi[h * RV : (h + 1) * RV]
                plo[k * H + h, at, n * L : (n + 1) * L] = lo[h * RV : (h + 1) * RV]
        return carry

    lax.fori_loop(0, R, p_split, 0)
    for v in range(NV):
        last_product(v)

    for n in range(NJ):
        out[0, n] = total[0:B, n * L : n * L + B]

    def sent(v, carry):
        def one(j, carry):
            a_copy(v, j + 1).wait_send()
            return carry

        lax.fori_loop(0, R - 1, one, 0)
        @pl.when(v < NV - DIRECT)
        def _():
            for i in range(1, Y):
                for h in range(2):
                    y_copy(v, i, h).wait_send()
            n_copy(v).wait_send()

            @pl.when(inner)
            def _():
                for u in range(2):
                    c_copy(v, u).wait_send()

            @pl.when(jnp.logical_not(inner))
            def _():
                f_copy(v).wait_send()

        @pl.when(v >= NV - DIRECT)
        def _():
            for step in range(1, R):
                m_copy(v, step).wait_send()

        for i in range(1, C):
            g_copy(v, i).wait_send()
        return carry

    lax.fori_loop(0, NV, sent, 0)
    for q in range(PARTS):
        p_near(q).wait_send()
        p_far(q).wait_send()

        @pl.when(inner)
        def _():
            for u in range(2):
                p_forward(u, q).wait_send()

        for zo in range(Z):
            for i in range(1, Y):
                p_across(zo, i, q).wait_send()


def shards(a_blocks, a_pattern, row_owner, prolong, p_pattern, prolong_slab):
    R, C = lax.axis_size("row"), lax.axis_size("col")
    W, KP, B = a_blocks.shape[:3]
    NA, NJ = prolong_slab.shape[1], prolong.shape[1]
    f32, bf16 = jnp.float32, jnp.bfloat16
    Y, NV, RV = R // Z, WAVES, KP * L // WAVES
    keep = R * NA <= 64
    slots = R if keep else 1
    oper = a_blocks.transpose(0, 2, 1, 3).reshape(W * B * KP, B)
    slab = prolong_slab.transpose(0, 2, 1, 3).reshape(W, B * NA, B)
    dma = pltpu.SemaphoreType.DMA
    vmem = pl.BlockSpec(memory_space=pltpu.VMEM)
    smem = pl.BlockSpec(memory_space=pltpu.SMEM)
    hbm = pl.BlockSpec(memory_space=pl.ANY)
    return pl.pallas_call(
        functools.partial(kernel, R, C, keep),
        out_shape=jax.ShapeDtypeStruct((1, NJ, B, B), f32),
        in_specs=[hbm, hbm, vmem, smem, smem, smem],
        out_specs=vmem,
        scratch_shapes=[
            pltpu.VMEM((W * B * KP, B), f32),
            pltpu.VMEM((W, B * NA, B), f32),
            pltpu.VMEM((CAP, L, L), f32),
            pltpu.VMEM((NV, R, CAP, RV, L), f32),
            pltpu.VMEM((NV, R, CAP, RV, L), f32),
            pltpu.VMEM((NA, L, L), f32),
            pltpu.VMEM((slots, NA // 2, CAP * L, 2 * L), bf16),
            pltpu.VMEM((slots, NA // 2, CAP * L, 2 * L), bf16),
            pltpu.VMEM((2 * RV, CAP * L), bf16),
            pltpu.VMEM((NV, Y, Z, RV, L), f32),
            pltpu.VMEM((NV, Y, Z, RV, L), f32),
            pltpu.VMEM((NV, Z, RV, L), f32),
            pltpu.VMEM((NV, 2, RV, L), f32),
            pltpu.VMEM((NV, RV, L), f32),
            pltpu.VMEM((NV, RV, L), f32),
            pltpu.VMEM((max(DIRECT, 1), R, RV, L), f32),
            pltpu.VMEM((NV, C * RV, L), f32),
            pltpu.VMEM((L, C * RV), bf16),
            pltpu.VMEM((L, C * RV), bf16),
            pltpu.VMEM((R, NJ, L, L), f32),
            pltpu.VMEM((NV, C * RV, NJ * L), bf16),
            pltpu.VMEM((NV, C * RV, NJ * L), bf16),
            pltpu.VMEM((L, NJ * L), f32),
            dma((2,)),
            dma((NV, R)), dma((NV, R)),
            dma((NV, Y, 2)), dma((NV, Y, 2)),
            dma((NV,)), dma((NV,)), dma((NV,)), dma((NV,)),
            dma((NV, 2)), dma((NV,)),
            dma((max(DIRECT, 1), R)), dma((max(DIRECT, 1), R)),
            dma((NV, C)), dma((NV, C)),
            dma((PARTS,)), dma((PARTS,)), dma((2, PARTS)), dma((Z, Y, PARTS)), dma((R, PARTS)),
        ],
        compiler_params=pltpu.CompilerParams(
            collective_id=0, has_side_effects=True, vmem_limit_bytes=VMEM_LIMIT
        ),
    )(oper, slab, prolong.transpose(1, 2, 0, 3), row_owner, a_pattern.T, p_pattern)


def solution(mesh):
    in_specs = (
        P("row", "col", None, None),
        P("row", "col"),
        P(),
        P("row", "col", None, None),
        P("row", "col"),
        P("row", None, None, None),
    )
    out_specs = P("row", "col", None, None)
    return jax.shard_map(shards, mesh=mesh, in_specs=in_specs, out_specs=out_specs, check_vma=False)
```

```python
import functools

import jax
import jax.numpy as jnp
from jax import lax
from jax.experimental import pallas as pl
from jax.experimental.pallas import tpu as pltpu
from jax.sharding import PartitionSpec as P

CAP = 2
Z = 4
L = 128
WAVES = 4
PARTS = 6
WINDOW = 0.25
DIRECT = 1
MESH = pl.DeviceIdType.MESH
VMEM_LIMIT = 58 * 1024 * 1024

SUMS = (0.2, 0.4, 0.6)
OWN = 0.02
LAST = 1.05
NEAR = 0.3
FAR = (0.05, 0.65)
INTO = 0.31
ONWARD = 0.15


def split(v):
    hi = v.astype(jnp.bfloat16)
    lo = (v - hi.astype(jnp.float32)).astype(jnp.bfloat16)
    return hi, lo


def dot(a, b):
    return jnp.dot(a, b, preferred_element_type=jnp.float32)


def kernel(
    R, C, KEEP, a_hbm, s_hbm, p_hbm, owner_hbm, a_pat_hbm, p_pat_hbm, out,
    a_v, p_in, owner, a_pat, p_pat, s_v, flip, asend, arecv, stage, sh, sl, ahl, macc, yrecv, nbuf, frecv, nrecv, crecv, mrecv,
    mfull, mth, mtl, pbuf, ph, plo, total,
    load, a_s, a_r, y_s, y_r, f_s, f_r, n_s, n_r, c_s, c_r, m_s, m_r, g_s, g_r, pn_s, pf_s, pw_s, py_s, p_r,
):
    KP, W, B = a_pat.shape[0], a_pat.shape[1], a_v.shape[1]
    NA, NJ = s_v.shape[1] // B, p_in.shape[0]
    NV, RV = WAVES, KP * L // WAVES
    H, Q = L // RV, NJ // PARTS
    Y = R // Z
    f32 = jnp.float32
    me, col = lax.axis_index("row"), lax.axis_index("col")
    z, y = lax.div(me, Y), lax.rem(me, Y)
    near0 = 2 * lax.div(z, 2)
    far0 = 2 - near0
    zn = 2 * near0 + 1 - z
    inner = (z == 1) | (z == 2)
    far_inner = jnp.where(z < 2, 2, 1)

    load_a = pltpu.make_async_copy(a_hbm, a_v, load.at[0])
    load_s = pltpu.make_async_copy(s_hbm, s_v, load.at[1])
    small = [
        pltpu.make_async_copy(src, dst, load.at[2 + i])
        for i, (src, dst) in enumerate(((owner_hbm, owner), (a_pat_hbm, a_pat), (p_pat_hbm, p_pat), (p_hbm, p_in)))
    ]
    load_a.start()
    for c in small:
        c.start()
    load_s.start()

    barrier = pltpu.get_barrier_semaphore()
    for i in range(1, R):
        pl.semaphore_signal(barrier, inc=1, device_id={"row": lax.rem(me + i, R)}, device_id_type=MESH)
    for i in range(1, C):
        pl.semaphore_signal(barrier, inc=1, device_id={"col": lax.rem(col + i, C)}, device_id_type=MESH)

    def pair(source, target):
        first, last = jnp.int32(W), jnp.int32(-1)
        for e in range(W):
            hit = lax.div(owner[source * W + e], W) == target
            first = jnp.minimum(first, jnp.where(hit, e, W))
            last = jnp.maximum(last, jnp.where(hit, e, -1))
        valid = last >= 0
        return (jnp.where(valid, first, 0), jnp.where(valid, last, 0)), valid

    def step_of(j):
        half = lax.div(j + 1, 2)
        return R // 2 + half * (1 - 2 * lax.rem(j, 2))

    def a_copy(v, step, act):
        def rows(count):
            at = pl.ds(0, count)
            act(pltpu.make_async_remote_copy(
                src_ref=asend.at[v, step, :, at], dst_ref=arecv.at[v, step, :, at],
                send_sem=a_s.at[v, step], recv_sem=a_r.at[v, step],
                device_id={"row": lax.rem(me + step, R)}, device_id_type=MESH,
            ))

        @pl.when(lax.rem(v, H) == H - 1)
        def _():
            rows(B - (H - 1) * RV)

        if H > 1:
            @pl.when(lax.rem(v, H) != H - 1)
            def _():
                rows(RV)

    def pack(buf, step, k):
        rows, valid = pair(me, lax.rem(me + step, R))
        for s in range(CAP):
            scale = jnp.where(valid, a_pat[k, rows[s]], 0).astype(f32)
            flip[s, 0:B, 0:B] = a_v[pl.ds(rows[s] * (B * KP) + k, B, stride=KP), :] * scale
        for s in range(CAP):
            turned = flip[s].T
            for h in range(H):
                buf[k * H + h, step, s] = turned[h * RV : (h + 1) * RV]

    def p_copy(slot, q, target, s_sem):
        at = pl.ds(q * Q, Q)
        return pltpu.make_async_remote_copy(
            src_ref=pbuf.at[slot, at, pl.ds(0, B)], dst_ref=pbuf.at[slot, at, pl.ds(0, B)], send_sem=s_sem, recv_sem=p_r.at[slot, q],
            device_id={"row": target}, device_id_type=MESH,
        )

    def p_near(q):
        return p_copy(me, q, zn * Y + y, pn_s.at[q])

    def p_far(q):
        return p_copy(me, q, far_inner * Y + y, pf_s.at[q])

    def p_forward(u, q):
        return p_copy((far0 + u) * Y + y, q, zn * Y + y, pw_s.at[u, q])

    def p_across(zo, i, q):
        return p_copy(zo * Y + y, q, z * Y + lax.rem(y + i, Y), py_s.at[zo, i, q])

    def p_arrived(slot, q):
        p_copy(slot, q, me, pn_s.at[q]).wait_recv()

    def all_across(zo, q):
        for i in range(1, Y):
            p_across(zo, i, q).start()

    def near_arrives(q):
        p_arrived(zn * Y + y, q)
        all_across(zn, q)

    def far_arrives(q):
        for u in range(2):
            p_arrived((far0 + u) * Y + y, q)

            @pl.when(inner)
            def _():
                p_forward(u, q).start()

            all_across(far0 + u, q)

    def y_copy(v, i, h):
        target = lax.rem(y + i, Y)
        at = pl.ds(near0 if h else far0, 2)
        return pltpu.make_async_remote_copy(
            src_ref=macc.at[v, target, at], dst_ref=yrecv.at[v, i, at], send_sem=y_s.at[v, i, h], recv_sem=y_r.at[v, i, h],
            device_id={"row": z * Y + target}, device_id_type=MESH,
        )

    def f_copy(v):
        return pltpu.make_async_remote_copy(
            src_ref=nbuf.at[v, pl.ds(far0, 2)], dst_ref=frecv.at[v], send_sem=f_s.at[v], recv_sem=f_r.at[v],
            device_id={"row": zn * Y + y}, device_id_type=MESH,
        )

    def n_copy(v):
        return pltpu.make_async_remote_copy(
            src_ref=nbuf.at[v, zn], dst_ref=nrecv.at[v], send_sem=n_s.at[v], recv_sem=n_r.at[v],
            device_id={"row": zn * Y + y}, device_id_type=MESH,
        )

    def c_copy(v, u):
        return pltpu.make_async_remote_copy(
            src_ref=nbuf.at[v, far0 + u], dst_ref=crecv.at[v], send_sem=c_s.at[v, u], recv_sem=c_r.at[v],
            device_id={"row": (far0 + u) * Y + y}, device_id_type=MESH,
        )

    def g_copy(v, i):
        at = pl.ds(pl.multiple_of(col * RV, RV), RV)
        return pltpu.make_async_remote_copy(
            src_ref=mfull.at[v, at], dst_ref=mfull.at[v, at], send_sem=g_s.at[v, i], recv_sem=g_r.at[v, i],
            device_id={"col": lax.rem(col + i, C)}, device_id_type=MESH,
        )

    def over_y(v):
        for h in range(2):
            for i in range(1, Y):
                y_copy(v, i, h).start()

    def over_near(v):
        for h in range(2):
            at = pl.ds(near0 if h else far0, 2)
            acc = macc[v, y, at]
            for i in range(1, Y):
                y_copy(v, i, h).wait_recv()
                acc += yrecv[v, i, at]
            nbuf[v, at] = acc
            if h == 0:
                @pl.when(jnp.logical_not(inner))
                def _():
                    f_copy(v).start()
            else:
                n_copy(v).start()

    def over_middle(v):
        @pl.when(inner)
        def _():
            f_copy(v).wait_recv()
            nbuf[v, pl.ds(far0, 2)] += frecv[v]
            for u in range(2):
                c_copy(v, u).start()

    def over_col(v):
        n_copy(v).wait_recv()
        c_copy(v, 0).wait_recv()
        mfull[v, pl.ds(pl.multiple_of(col * RV, RV), RV)] = nbuf[v, z] + nrecv[v] + crecv[v]
        for i in range(1, C):
            g_copy(v, i).start()

    def m_copy(v, step):
        target = lax.rem(me + step, R)
        d = jnp.maximum(v - (NV - DIRECT), 0)
        return pltpu.make_async_remote_copy(
            src_ref=macc.at[v, lax.rem(target, Y), lax.div(target, Y)], dst_ref=mrecv.at[d, step],
            send_sem=m_s.at[d, step], recv_sem=m_r.at[d, step],
            device_id={"row": target}, device_id_type=MESH,
        )

    def over_rows(v):
        def one(j, carry):
            m_copy(v, step_of(j)).start()
            return carry

        lax.fori_loop(0, R - 1, one, 0)

    def col_after_rows(v):
        acc = macc[v, y, z]
        for step in range(1, R):
            m_copy(v, step).wait_recv()
            acc += mrecv[v - (NV - DIRECT), step]
        mfull[v, pl.ds(pl.multiple_of(col * RV, RV), RV)] = acc
        for i in range(1, C):
            g_copy(v, i).start()

    def last_product(v):
        for i in range(1, C):
            g_copy(v, i).wait_recv()
        for c in range(C * RV // L):
            hi, lo = split(mfull[v, c * L : (c + 1) * L].T)
            mth[:, c * L : (c + 1) * L] = hi
            mtl[:, c * L : (c + 1) * L] = lo
        total[...] += dot(mth[...], ph[v]) + (dot(mth[...], plo[v]) + dot(mtl[...], ph[v]))

    flip[...] = jnp.zeros_like(flip)
    pad = H * RV - B
    for k in range(KP):
        arecv[k * H + H - 1, :, :, RV - pad : RV] = jnp.zeros((R, CAP, pad, L), f32)
    pbuf[:, :, B:L] = jnp.zeros((R, NJ, L - B, L), f32)
    for c in small:
        c.wait()
    load_a.wait()

    def first_pack(j, carry):
        pack(asend, step_of(j), 0)
        return carry

    lax.fori_loop(0, R - 1, first_pack, 0)
    pl.semaphore_wait(barrier, R + C - 2)

    def send(n, carry):
        a_copy(lax.div(n, R - 1), step_of(lax.rem(n, R - 1)), lambda c: c.start())
        return carry

    window = min(int(WINDOW * NV * R), H * (R - 1))
    lax.fori_loop(0, window, send, 0)

    for k in range(1, KP):
        def later_pack(j, carry):
            pack(asend, step_of(j), k)
            return carry

        lax.fori_loop(0, R - 1, later_pack, 0)

    for n in range(NJ):
        pbuf[me, n] = jnp.zeros((L, L), f32)
        pbuf[me, n, 0:B, 0:B] = p_in[n, :, 0, :] * p_pat[0, n].astype(f32)
    for k in range(KP):
        pack(arecv, 0, k)
    stage[...] = jnp.zeros_like(stage)
    macc[...] = jnp.zeros_like(macc)
    total[...] = jnp.zeros_like(total)
    load_s.wait()

    def slab(step, keep):
        source = lax.rem(me - step + R, R)
        rows, valid = pair(source, me)
        for s in range(CAP):
            g = jnp.where(valid, owner[source * W + rows[s]] - me * W, 0)

            def one(b, carry):
                for h in range(2):
                    stage[2 * b + h, 0:B, 0:B] = s_v[g, pl.ds(2 * b + h, B, stride=NA), :]
                for h in range(2):
                    hi, lo = split(stage[2 * b + h])
                    sh[keep, b, s * L : (s + 1) * L, h * L : (h + 1) * L] = hi
                    sl[keep, b, s * L : (s + 1) * L, h * L : (h + 1) * L] = lo
                return carry

            lax.fori_loop(0, NA // 2, one, 0)

    def work(t, carry):
        v, j = lax.div(t, R), lax.rem(t, R)
        step = jnp.where(j == 0, 0, step_of(j - 1))
        keep = step if KEEP else 0
        if KEEP:
            @pl.when(v == 0)
            def _():
                slab(step, step)
        else:
            slab(step, 0)

        @pl.when(j > 0)
        def _():
            a_copy(v, step, lambda c: c.wait_recv())
            ahead = v * (R - 1) + j - 1 + window

            @pl.when(ahead < NV * (R - 1))
            def _():
                send(ahead, 0)

        for s in range(CAP):
            hi, lo = split(arecv[v, step, s])
            ahl[0:RV, s * L : (s + 1) * L] = hi
            ahl[RV : 2 * RV, s * L : (s + 1) * L] = lo
        for b in range(NA // 2):
            both = dot(ahl[...], sh[keep, b])
            r = both[0:RV] + (both[RV : 2 * RV] + dot(ahl[0:RV], sl[keep, b]))
            for h in range(2):
                a = 2 * b + h
                macc[v, a % Y, a // Y] += r[:, h * L : (h + 1) * L]

        @pl.when((j == R - 1) & (v < NV - DIRECT))
        def _():
            over_y(v)

        @pl.when((j == R - 1) & (v >= NV - DIRECT))
        def _():
            over_rows(v)

        for when, act in todo:
            if when < NV * R:
                pl.when(t == when)(act)
        return carry

    def own_starts():
        for q in range(PARTS):
            p_near(q).start()
            all_across(z, q)

    def near_comes():
        for q in range(PARTS):
            near_arrives(q)

    def place(when):
        return int(when * NV * R)

    todo = [(place(OWN), own_starts), (place(NEAR), near_comes)]
    for q in range(PARTS):
        far = FAR[0] + (FAR[1] - FAR[0]) * q / max(PARTS - 1, 1)
        todo.append((place(far), lambda q=q: p_far(q).start()))
        todo.append((place(far + INTO), lambda q=q: pl.when(inner)(lambda: far_arrives(q))))
        todo.append((place(far + INTO + ONWARD), lambda q=q: pl.when(jnp.logical_not(inner))(lambda: far_arrives(q))))
    for v in range(NV - DIRECT):
        for d, act in enumerate((over_near, over_middle, over_col)):
            todo.append(((v + 1) * R - 1 + place(SUMS[d]), lambda v=v, act=act: act(v)))
    for v in range(NV - DIRECT, NV):
        todo.append((max(place(LAST), NV * R), lambda v=v: col_after_rows(v)))
    todo.sort(key=lambda item: item[0])

    lax.fori_loop(0, NV * R, work, 0)
    for when, act in todo:
        if when >= NV * R:
            act()

    for q in range(PARTS):
        for zo in range(Z):
            for i in range(1, Y):
                p_arrived(zo * Y + lax.rem(y + i, Y), q)

    def p_split(r, carry):
        c, k = lax.div(r, KP), lax.rem(r, KP)
        at = pl.ds(pl.multiple_of(c * RV, RV), RV)
        for n in range(NJ):
            hi, lo = split(pbuf[r, n])
            for h in range(H):
                ph[k * H + h, at, n * L : (n + 1) * L] = hi[h * RV : (h + 1) * RV]
                plo[k * H + h, at, n * L : (n + 1) * L] = lo[h * RV : (h + 1) * RV]
        return carry

    lax.fori_loop(0, R, p_split, 0)
    for v in range(NV):
        last_product(v)

    for n in range(NJ):
        out[0, n] = total[0:B, n * L : n * L + B]

    def sent(v, carry):
        def one(j, carry):
            a_copy(v, j + 1, lambda c: c.wait_send())
            return carry

        lax.fori_loop(0, R - 1, one, 0)
        @pl.when(v < NV - DIRECT)
        def _():
            for i in range(1, Y):
                for h in range(2):
                    y_copy(v, i, h).wait_send()
            n_copy(v).wait_send()

            @pl.when(inner)
            def _():
                for u in range(2):
                    c_copy(v, u).wait_send()

            @pl.when(jnp.logical_not(inner))
            def _():
                f_copy(v).wait_send()

        @pl.when(v >= NV - DIRECT)
        def _():
            for step in range(1, R):
                m_copy(v, step).wait_send()

        for i in range(1, C):
            g_copy(v, i).wait_send()
        return carry

    lax.fori_loop(0, NV, sent, 0)
    for q in range(PARTS):
        p_near(q).wait_send()
        p_far(q).wait_send()

        @pl.when(inner)
        def _():
            for u in range(2):
                p_forward(u, q).wait_send()

        for zo in range(Z):
            for i in range(1, Y):
                p_across(zo, i, q).wait_send()


def shards(a_blocks, a_pattern, row_owner, prolong, p_pattern, prolong_slab):
    R, C = lax.axis_size("row"), lax.axis_size("col")
    W, KP, B = a_blocks.shape[:3]
    NA, NJ = prolong_slab.shape[1], prolong.shape[1]
    f32, bf16 = jnp.float32, jnp.bfloat16
    Y, NV, RV = R // Z, WAVES, KP * L // WAVES
    keep = R * NA <= 64
    slots = R if keep else 1
    oper = a_blocks.transpose(0, 2, 1, 3).reshape(W * B * KP, B)
    slab = prolong_slab.transpose(0, 2, 1, 3).reshape(W, B * NA, B)
    dma = pltpu.SemaphoreType.DMA
    vmem = pl.BlockSpec(memory_space=pltpu.VMEM)
    hbm = pl.BlockSpec(memory_space=pl.ANY)
    return pl.pallas_call(
        functools.partial(kernel, R, C, keep),
        out_shape=jax.ShapeDtypeStruct((1, NJ, B, B), f32),
        in_specs=[hbm] * 6,
        out_specs=vmem,
        scratch_shapes=[
            pltpu.VMEM((W * B * KP, B), f32),
            pltpu.VMEM((NJ, B, 1, B), f32),
            pltpu.SMEM(row_owner.shape, jnp.int32),
            pltpu.SMEM((KP, W), jnp.int32),
            pltpu.SMEM((1, NJ), jnp.int32),
            pltpu.VMEM((W, B * NA, B), f32),
            pltpu.VMEM((CAP, L, L), f32),
            pltpu.VMEM((NV, R, CAP, RV, L), f32),
            pltpu.VMEM((NV, R, CAP, RV, L), f32),
            pltpu.VMEM((NA, L, L), f32),
            pltpu.VMEM((slots, NA // 2, CAP * L, 2 * L), bf16),
            pltpu.VMEM((slots, NA // 2, CAP * L, 2 * L), bf16),
            pltpu.VMEM((2 * RV, CAP * L), bf16),
            pltpu.VMEM((NV, Y, Z, RV, L), f32),
            pltpu.VMEM((NV, Y, Z, RV, L), f32),
            pltpu.VMEM((NV, Z, RV, L), f32),
            pltpu.VMEM((NV, 2, RV, L), f32),
            pltpu.VMEM((NV, RV, L), f32),
            pltpu.VMEM((NV, RV, L), f32),
            pltpu.VMEM((max(DIRECT, 1), R, RV, L), f32),
            pltpu.VMEM((NV, C * RV, L), f32),
            pltpu.VMEM((L, C * RV), bf16),
            pltpu.VMEM((L, C * RV), bf16),
            pltpu.VMEM((R, NJ, L, L), f32),
            pltpu.VMEM((NV, C * RV, NJ * L), bf16),
            pltpu.VMEM((NV, C * RV, NJ * L), bf16),
            pltpu.VMEM((L, NJ * L), f32),
            dma((6,)),
            dma((NV, R)), dma((NV, R)),
            dma((NV, Y, 2)), dma((NV, Y, 2)),
            dma((NV,)), dma((NV,)), dma((NV,)), dma((NV,)),
            dma((NV, 2)), dma((NV,)),
            dma((max(DIRECT, 1), R)), dma((max(DIRECT, 1), R)),
            dma((NV, C)), dma((NV, C)),
            dma((PARTS,)), dma((PARTS,)), dma((2, PARTS)), dma((Z, Y, PARTS)), dma((R, PARTS)),
        ],
        compiler_params=pltpu.CompilerParams(
            collective_id=0, has_side_effects=True, vmem_limit_bytes=VMEM_LIMIT
        ),
    )(oper, slab, prolong.transpose(1, 2, 0, 3), row_owner, a_pattern.T, p_pattern)


def solution(mesh):
    in_specs = (
        P("row", "col", None, None),
        P("row", "col"),
        P(),
        P("row", "col", None, None),
        P("row", "col"),
        P("row", None, None, None),
    )
    out_specs = P("row", "col", None, None)
    return jax.shard_map(shards, mesh=mesh, in_specs=in_specs, out_specs=out_specs, check_vma=False)
```

```python
import functools

import jax
import jax.numpy as jnp
from jax import lax
from jax.experimental import pallas as pl
from jax.experimental.pallas import tpu as pltpu
from jax.sharding import PartitionSpec as P

CAP = 2
Z = 4
L = 128
CUTS = (128,)
SMALL_CUTS = (64, 64)
LAST_CUTS = (64, 64)
PARTS = 6
WINDOW = (6, 10, 12)
DIRECT = 0
MESH = pl.DeviceIdType.MESH
VMEM_LIMIT = 58 * 1024 * 1024

SUMS = (0.2, 0.4, 0.6)
OWN = 0.02
LAST = 1.05
NEAR = 0.3
FAR = (0.05, 0.75)
INTO = 0.31
ONWARD = 0.15


def waves_of(KP, roomy):
    waves = []
    for k in range(KP):
        first = 0
        for rows in LAST_CUTS if k == KP - 1 else CUTS if roomy else SMALL_CUTS:
            waves.append((k, first, rows))
            first += rows
    return waves


def split(v):
    hi = v.astype(jnp.bfloat16)
    lo = (v - hi.astype(jnp.float32)).astype(jnp.bfloat16)
    return hi, lo


def dot(a, b):
    return jnp.dot(a, b, preferred_element_type=jnp.float32)


def kernel(
    R, C, KEEP, a_hbm, s_hbm, p_hbm, owner_hbm, a_pat_hbm, p_pat_hbm, out,
    a_v, p_in, owner, a_pat, p_pat, s_v, flip, asend, arecv, stage, sh, sl, ahl, macc, yrecv, nbuf, frecv, nrecv, crecv, mrecv,
    mfull, mth, mtl, pbuf, ph, plo, total,
    load, a_s, a_r, y_s, y_r, f_s, f_r, n_s, n_r, c_s, c_r, m_s, m_r, g_s, g_r, pn_s, pf_s, pw_s, py_s, p_r,
):
    KP, W, B = a_pat.shape[0], a_pat.shape[1], a_v.shape[1]
    NA, NJ = s_v.shape[1] // B, p_in.shape[0]
    waves = waves_of(KP, KEEP)
    NV, Q = len(waves), NJ // PARTS
    window = [WINDOW[min(v, len(WINDOW) - 1)] * R // 8 for v in range(NV)]
    Y = R // Z
    f32 = jnp.float32
    me, col = lax.axis_index("row"), lax.axis_index("col")
    z, y = lax.div(me, Y), lax.rem(me, Y)
    near0 = 2 * lax.div(z, 2)
    far0 = 2 - near0
    zn = 2 * near0 + 1 - z
    inner = (z == 1) | (z == 2)
    far_inner = jnp.where(z < 2, 2, 1)

    load_a = pltpu.make_async_copy(a_hbm, a_v, load.at[0])
    load_s = pltpu.make_async_copy(s_hbm, s_v, load.at[1])
    small = [
        pltpu.make_async_copy(src, dst, load.at[2 + i])
        for i, (src, dst) in enumerate(((owner_hbm, owner), (a_pat_hbm, a_pat), (p_pat_hbm, p_pat), (p_hbm, p_in)))
    ]
    load_a.start()
    for c in small:
        c.start()
    load_s.start()

    barrier = pltpu.get_barrier_semaphore()
    for i in range(1, R):
        pl.semaphore_signal(barrier, inc=1, device_id={"row": lax.rem(me + i, R)}, device_id_type=MESH)
    for i in range(1, C):
        pl.semaphore_signal(barrier, inc=1, device_id={"col": lax.rem(col + i, C)}, device_id_type=MESH)

    def pair(source, target):
        first, last = jnp.int32(W), jnp.int32(-1)
        for e in range(W):
            hit = lax.div(owner[source * W + e], W) == target
            first = jnp.minimum(first, jnp.where(hit, e, W))
            last = jnp.maximum(last, jnp.where(hit, e, -1))
        valid = last >= 0
        return (jnp.where(valid, first, 0), jnp.where(valid, last, 0)), valid

    def step_of(j):
        half = lax.div(j + 1, 2)
        return R // 2 + half * (1 - 2 * lax.rem(j, 2))

    def a_copy(v, step):
        at = pl.ds(0, min(waves[v][2], B - waves[v][1]))
        return pltpu.make_async_remote_copy(
            src_ref=asend.at[v, step, :, at], dst_ref=arecv.at[v, step, :, at],
            send_sem=a_s.at[v, step], recv_sem=a_r.at[v, step],
            device_id={"row": lax.rem(me + step, R)}, device_id_type=MESH,
        )

    def pack(buf, step, k):
        chosen, valid = pair(me, lax.rem(me + step, R))
        for s in range(CAP):
            scale = jnp.where(valid, a_pat[k, chosen[s]], 0).astype(f32)
            flip[s, 0:B, 0:B] = a_v[pl.ds(chosen[s] * (B * KP) + k, B, stride=KP), :] * scale
        for s in range(CAP):
            turned = flip[s].T
            for v, (block, first, rows) in enumerate(waves):
                if block == k:
                    buf[v, step, s, 0:rows] = turned[first : first + rows]

    def p_copy(slot, q, target, s_sem):
        at = pl.ds(q * Q, Q)
        return pltpu.make_async_remote_copy(
            src_ref=pbuf.at[slot, at, pl.ds(0, B)], dst_ref=pbuf.at[slot, at, pl.ds(0, B)], send_sem=s_sem, recv_sem=p_r.at[slot, q],
            device_id={"row": target}, device_id_type=MESH,
        )

    def p_near(q):
        return p_copy(me, q, zn * Y + y, pn_s.at[q])

    def p_far(q):
        return p_copy(me, q, far_inner * Y + y, pf_s.at[q])

    def p_forward(u, q):
        return p_copy((far0 + u) * Y + y, q, zn * Y + y, pw_s.at[u, q])

    def p_across(zo, i, q):
        return p_copy(zo * Y + y, q, z * Y + lax.rem(y + i, Y), py_s.at[zo, i, q])

    def p_arrived(slot, q):
        p_copy(slot, q, me, pn_s.at[q]).wait_recv()

    def all_across(zo, q):
        for i in range(1, Y):
            p_across(zo, i, q).start()

    def near_arrives(q):
        p_arrived(zn * Y + y, q)
        all_across(zn, q)

    def far_arrives(q):
        for u in range(2):
            p_arrived((far0 + u) * Y + y, q)

            @pl.when(inner)
            def _():
                p_forward(u, q).start()

            all_across(far0 + u, q)

    def tall(v):
        return pl.ds(0, waves[v][2])

    def mine(v):
        rows = waves[v][2]
        return pl.ds(pl.multiple_of(col * rows, rows), rows)

    def y_copy(v, i, h):
        target = lax.rem(y + i, Y)
        at = pl.ds(near0 if h else far0, 2)
        return pltpu.make_async_remote_copy(
            src_ref=macc.at[v, target, at, tall(v)], dst_ref=yrecv.at[v, i, at, tall(v)], send_sem=y_s.at[v, i, h], recv_sem=y_r.at[v, i, h],
            device_id={"row": z * Y + target}, device_id_type=MESH,
        )

    def f_copy(v):
        return pltpu.make_async_remote_copy(
            src_ref=nbuf.at[v, pl.ds(far0, 2), tall(v)], dst_ref=frecv.at[v, :, tall(v)], send_sem=f_s.at[v], recv_sem=f_r.at[v],
            device_id={"row": zn * Y + y}, device_id_type=MESH,
        )

    def n_copy(v):
        return pltpu.make_async_remote_copy(
            src_ref=nbuf.at[v, zn, tall(v)], dst_ref=nrecv.at[v, tall(v)], send_sem=n_s.at[v], recv_sem=n_r.at[v],
            device_id={"row": zn * Y + y}, device_id_type=MESH,
        )

    def c_copy(v, u):
        return pltpu.make_async_remote_copy(
            src_ref=nbuf.at[v, far0 + u, tall(v)], dst_ref=crecv.at[v, tall(v)], send_sem=c_s.at[v, u], recv_sem=c_r.at[v],
            device_id={"row": (far0 + u) * Y + y}, device_id_type=MESH,
        )

    def g_copy(v, i):
        at = mine(v)
        return pltpu.make_async_remote_copy(
            src_ref=mfull.at[v, at], dst_ref=mfull.at[v, at], send_sem=g_s.at[v, i], recv_sem=g_r.at[v, i],
            device_id={"col": lax.rem(col + i, C)}, device_id_type=MESH,
        )

    def over_y(v):
        for h in range(2):
            for i in range(1, Y):
                y_copy(v, i, h).start()

    def over_near(v):
        for h in range(2):
            at = pl.ds(near0 if h else far0, 2)
            acc = macc[v, y, at, tall(v)]
            for i in range(1, Y):
                y_copy(v, i, h).wait_recv()
                acc += yrecv[v, i, at, tall(v)]
            nbuf[v, at, tall(v)] = acc
            if h == 0:
                @pl.when(jnp.logical_not(inner))
                def _():
                    f_copy(v).start()
            else:
                n_copy(v).start()

    def over_middle(v):
        @pl.when(inner)
        def _():
            f_copy(v).wait_recv()
            nbuf[v, pl.ds(far0, 2), tall(v)] += frecv[v, :, tall(v)]
            for u in range(2):
                c_copy(v, u).start()

    def over_col(v):
        n_copy(v).wait_recv()
        c_copy(v, 0).wait_recv()
        mfull[v, mine(v)] = nbuf[v, z, tall(v)] + nrecv[v, tall(v)] + crecv[v, tall(v)]
        for i in range(1, C):
            g_copy(v, i).start()

    def m_copy(v, step):
        target = lax.rem(me + step, R)
        d = v - (NV - DIRECT)
        return pltpu.make_async_remote_copy(
            src_ref=macc.at[v, lax.rem(target, Y), lax.div(target, Y), tall(v)], dst_ref=mrecv.at[d, step, tall(v)],
            send_sem=m_s.at[d, step], recv_sem=m_r.at[d, step],
            device_id={"row": target}, device_id_type=MESH,
        )

    def over_rows(v):
        def one(j, carry):
            m_copy(v, step_of(j)).start()
            return carry

        lax.fori_loop(0, R - 1, one, 0)

    def col_after_rows(v):
        acc = macc[v, y, z, tall(v)]
        for step in range(1, R):
            m_copy(v, step).wait_recv()
            acc += mrecv[v - (NV - DIRECT), step, tall(v)]
        mfull[v, mine(v)] = acc
        for i in range(1, C):
            g_copy(v, i).start()

    def last_product(v):
        for i in range(1, C):
            g_copy(v, i).wait_recv()
        width = C * waves[v][2]
        for c in range(width // L):
            hi, lo = split(mfull[v, c * L : (c + 1) * L].T)
            mth[:, c * L : (c + 1) * L] = hi
            mtl[:, c * L : (c + 1) * L] = lo
        mh, ml, fh = mth[:, 0:width], mtl[:, 0:width], ph[v, 0:width]
        total[...] += dot(mh, fh) + (dot(mh, plo[v, 0:width]) + dot(ml, fh))

    flip[...] = jnp.zeros_like(flip)
    for v, (block, first, rows) in enumerate(waves):
        if first + rows > B:
            arecv[v, :, :, B - first : rows] = jnp.zeros((R, CAP, first + rows - B, L), f32)
    pbuf[:, :, B:L] = jnp.zeros((R, NJ, L - B, L), f32)
    for c in small:
        c.wait()
    load_a.wait()

    def first_pack(j, carry):
        pack(asend, step_of(j), 0)
        return carry

    lax.fori_loop(0, R - 1, first_pack, 0)
    pl.semaphore_wait(barrier, R + C - 2)

    def send(n):
        if n < NV * (R - 1):
            a_copy(n // (R - 1), step_of(jnp.int32(n % (R - 1)))).start()

    for n in range(window[0]):
        send(n)

    for k in range(1, KP):
        def later_pack(j, carry):
            pack(asend, step_of(j), k)
            return carry

        lax.fori_loop(0, R - 1, later_pack, 0)

    for n in range(NJ):
        pbuf[me, n] = jnp.zeros((L, L), f32)
        pbuf[me, n, 0:B, 0:B] = p_in[n, :, 0, :] * p_pat[0, n].astype(f32)
    for k in range(KP):
        pack(arecv, 0, k)
    stage[...] = jnp.zeros_like(stage)
    macc[...] = jnp.zeros_like(macc)
    total[...] = jnp.zeros_like(total)
    load_s.wait()

    def slab(step, keep):
        source = lax.rem(me - step + R, R)
        rows, valid = pair(source, me)
        for s in range(CAP):
            g = jnp.where(valid, owner[source * W + rows[s]] - me * W, 0)

            def one(b, carry):
                for h in range(2):
                    stage[2 * b + h, 0:B, 0:B] = s_v[g, pl.ds(2 * b + h, B, stride=NA), :]
                for h in range(2):
                    hi, lo = split(stage[2 * b + h])
                    sh[keep, b, s * L : (s + 1) * L, h * L : (h + 1) * L] = hi
                    sl[keep, b, s * L : (s + 1) * L, h * L : (h + 1) * L] = lo
                return carry

            lax.fori_loop(0, NA // 2, one, 0)

    def work(v, j, carry):
        rows = waves[v][2]
        step = jnp.where(j == 0, 0, step_of(j - 1))
        keep = step if KEEP else 0
        if v == 0 or not KEEP:
            slab(step, keep)

        @pl.when(j > 0)
        def _():
            a_copy(v, step).wait_recv()
            for other in range(v, NV):
                ahead = j - 1 + window[v] - (other - v) * (R - 1)

                @pl.when((ahead >= 0) & (ahead < R - 1))
                def _():
                    a_copy(other, step_of(ahead)).start()

        for s in range(CAP):
            hi, lo = split(arecv[v, step, s, tall(v)])
            ahl[0:rows, s * L : (s + 1) * L] = hi
            ahl[rows : 2 * rows, s * L : (s + 1) * L] = lo
        for b in range(NA // 2):
            both = dot(ahl[0 : 2 * rows], sh[keep, b])
            r = both[0:rows] + (both[rows : 2 * rows] + dot(ahl[0:rows], sl[keep, b]))
            for h in range(2):
                a = 2 * b + h
                macc[v, a % Y, a // Y, tall(v)] += r[:, h * L : (h + 1) * L]

        @pl.when(j == R - 1)
        def _():
            (over_y if v < NV - DIRECT else over_rows)(v)

        for when, act in todo:
            if when // R == v:
                pl.when(j == when % R)(act)
        return carry

    def own_starts():
        for q in range(PARTS):
            p_near(q).start()
            all_across(z, q)

    def near_comes():
        for q in range(PARTS):
            near_arrives(q)

    ends = []
    for v, (_, _, rows) in enumerate(waves):
        start = ends[-1] if ends else 0.0
        ends += [start + rows * (j + 1) / (R * KP * L) for j in range(R)]

    def place(when):
        for t, end in enumerate(ends):
            if when <= end:
                return t
        return NV * R + int((when - 1) * 1000)

    todo = [(place(OWN), own_starts), (place(NEAR), near_comes)]
    for q in range(PARTS):
        far = FAR[0] + (FAR[1] - FAR[0]) * q / max(PARTS - 1, 1)
        todo.append((place(far), lambda q=q: p_far(q).start()))
        todo.append((place(far + INTO), lambda q=q: pl.when(inner)(lambda: far_arrives(q))))
        todo.append((place(far + INTO + ONWARD), lambda q=q: pl.when(jnp.logical_not(inner))(lambda: far_arrives(q))))
    for v in range(NV - DIRECT):
        for d, act in enumerate((over_near, over_middle, over_col)):
            todo.append((place(ends[(v + 1) * R - 1] + SUMS[d]), lambda v=v, act=act: act(v)))
    for v in range(NV - DIRECT, NV):
        todo.append((max(place(LAST), NV * R), lambda v=v: col_after_rows(v)))
    todo.sort(key=lambda item: item[0])

    for v in range(NV):
        if v > 0:
            for n in range(window[v - 1], window[v]):
                send(v * (R - 1) + n)
        lax.fori_loop(0, R, functools.partial(work, v), 0)
    for when, act in todo:
        if when >= NV * R:
            act()

    for q in range(PARTS):
        for zo in range(Z):
            for i in range(1, Y):
                p_arrived(zo * Y + lax.rem(y + i, Y), q)

    def p_split(c, carry):
        for k in range(KP):
            for n in range(NJ):
                hi, lo = split(pbuf[c * KP + k, n])
                for v, (block, first, rows) in enumerate(waves):
                    if block == k:
                        at = pl.ds(pl.multiple_of(c * rows, rows), rows)
                        ph[v, at, n * L : (n + 1) * L] = hi[first : first + rows]
                        plo[v, at, n * L : (n + 1) * L] = lo[first : first + rows]
        return carry

    lax.fori_loop(0, C, p_split, 0)
    for v in range(NV):
        last_product(v)

    for n in range(NJ):
        out[0, n] = total[0:B, n * L : n * L + B]

    for v in range(NV):
        def sent(j, carry):
            a_copy(v, j + 1).wait_send()
            return carry

        lax.fori_loop(0, R - 1, sent, 0)
        if v < NV - DIRECT:
            for i in range(1, Y):
                for h in range(2):
                    y_copy(v, i, h).wait_send()
            n_copy(v).wait_send()

            @pl.when(inner)
            def _():
                for u in range(2):
                    c_copy(v, u).wait_send()

            @pl.when(jnp.logical_not(inner))
            def _():
                f_copy(v).wait_send()
        else:
            for step in range(1, R):
                m_copy(v, step).wait_send()
        for i in range(1, C):
            g_copy(v, i).wait_send()
    for q in range(PARTS):
        p_near(q).wait_send()
        p_far(q).wait_send()

        @pl.when(inner)
        def _():
            for u in range(2):
                p_forward(u, q).wait_send()

        for zo in range(Z):
            for i in range(1, Y):
                p_across(zo, i, q).wait_send()


def shards(a_blocks, a_pattern, row_owner, prolong, p_pattern, prolong_slab):
    R, C = lax.axis_size("row"), lax.axis_size("col")
    W, KP, B = a_blocks.shape[:3]
    NA, NJ = prolong_slab.shape[1], prolong.shape[1]
    f32, bf16 = jnp.float32, jnp.bfloat16
    keep = R * NA <= 64
    waves = waves_of(KP, keep)
    Y, NV, RV = R // Z, len(waves), max(rows for _, _, rows in waves)
    slots = R if keep else 1
    oper = a_blocks.transpose(0, 2, 1, 3).reshape(W * B * KP, B)
    slab = prolong_slab.transpose(0, 2, 1, 3).reshape(W, B * NA, B)
    dma = pltpu.SemaphoreType.DMA
    vmem = pl.BlockSpec(memory_space=pltpu.VMEM)
    hbm = pl.BlockSpec(memory_space=pl.ANY)
    return pl.pallas_call(
        functools.partial(kernel, R, C, keep),
        out_shape=jax.ShapeDtypeStruct((1, NJ, B, B), f32),
        in_specs=[hbm] * 6,
        out_specs=vmem,
        scratch_shapes=[
            pltpu.VMEM((W * B * KP, B), f32),
            pltpu.VMEM((NJ, B, 1, B), f32),
            pltpu.SMEM(row_owner.shape, jnp.int32),
            pltpu.SMEM((KP, W), jnp.int32),
            pltpu.SMEM((1, NJ), jnp.int32),
            pltpu.VMEM((W, B * NA, B), f32),
            pltpu.VMEM((CAP, L, L), f32),
            pltpu.VMEM((NV, R, CAP, RV, L), f32),
            pltpu.VMEM((NV, R, CAP, RV, L), f32),
            pltpu.VMEM((NA, L, L), f32),
            pltpu.VMEM((slots, NA // 2, CAP * L, 2 * L), bf16),
            pltpu.VMEM((slots, NA // 2, CAP * L, 2 * L), bf16),
            pltpu.VMEM((2 * RV, CAP * L), bf16),
            pltpu.VMEM((NV, Y, Z, RV, L), f32),
            pltpu.VMEM((NV, Y, Z, RV, L), f32),
            pltpu.VMEM((NV, Z, RV, L), f32),
            pltpu.VMEM((NV, 2, RV, L), f32),
            pltpu.VMEM((NV, RV, L), f32),
            pltpu.VMEM((NV, RV, L), f32),
            pltpu.VMEM((max(DIRECT, 1), R, RV, L), f32),
            pltpu.VMEM((NV, C * RV, L), f32),
            pltpu.VMEM((L, C * RV), bf16),
            pltpu.VMEM((L, C * RV), bf16),
            pltpu.VMEM((R, NJ, L, L), f32),
            pltpu.VMEM((NV, C * RV, NJ * L), bf16),
            pltpu.VMEM((NV, C * RV, NJ * L), bf16),
            pltpu.VMEM((L, NJ * L), f32),
            dma((6,)),
            dma((NV, R)), dma((NV, R)),
            dma((NV, Y, 2)), dma((NV, Y, 2)),
            dma((NV,)), dma((NV,)), dma((NV,)), dma((NV,)),
            dma((NV, 2)), dma((NV,)),
            dma((max(DIRECT, 1), R)), dma((max(DIRECT, 1), R)),
            dma((NV, C)), dma((NV, C)),
            dma((PARTS,)), dma((PARTS,)), dma((2, PARTS)), dma((Z, Y, PARTS)), dma((R, PARTS)),
        ],
        compiler_params=pltpu.CompilerParams(
            collective_id=0, has_side_effects=True, vmem_limit_bytes=VMEM_LIMIT
        ),
    )(oper, slab, prolong.transpose(1, 2, 0, 3), row_owner, a_pattern.T, p_pattern)


def solution(mesh):
    in_specs = (
        P("row", "col", None, None),
        P("row", "col"),
        P(),
        P("row", "col", None, None),
        P("row", "col"),
        P("row", None, None, None),
    )
    out_specs = P("row", "col", None, None)
    return jax.shard_map(shards, mesh=mesh, in_specs=in_specs, out_specs=out_specs, check_vma=False)
```

```python
import functools

import jax
import jax.numpy as jnp
from jax import lax
from jax.experimental import pallas as pl
from jax.experimental.pallas import tpu as pltpu
from jax.sharding import PartitionSpec as P

CAP = 2
Z = 4
L = 128
CUTS = (128,)
SMALL_CUTS = (64, 64)
LAST_CUTS = (64, 64)
PARTS = 6
WINDOW = (7, 12, 14)
DIRECT = 0
MESH = pl.DeviceIdType.MESH
VMEM_LIMIT = 58 * 1024 * 1024

SUMS = (0.2, 0.4, 0.6)
OWN = 0.02
LAST = 1.05
NEAR = 0.3
FAR = (0.05, 0.75)
INTO = 0.31
ONWARD = 0.15


def waves_of(KP, roomy):
    waves = []
    for k in range(KP):
        first = 0
        for rows in LAST_CUTS if k == KP - 1 else CUTS if roomy else SMALL_CUTS:
            waves.append((k, first, rows))
            first += rows
    return waves


def split(v):
    hi = v.astype(jnp.bfloat16)
    lo = (v - hi.astype(jnp.float32)).astype(jnp.bfloat16)
    return hi, lo


def dot(a, b):
    return jnp.dot(a, b, preferred_element_type=jnp.float32)


def kernel(
    R, C, KEEP, a_hbm, s_hbm, p_hbm, owner_hbm, a_pat_hbm, p_pat_hbm, out,
    a_v, p_in, owner, a_pat, p_pat, s_v, flip, asend, arecv, stage, sh, sl, ahl, macc, yrecv, nbuf, frecv, nrecv, crecv, mrecv,
    mfull, mth, mtl, pbuf, ph, plo, total,
    load, a_s, a_r, y_s, y_r, f_s, f_r, n_s, n_r, c_s, c_r, m_s, m_r, g_s, g_r, pn_s, pf_s, pw_s, py_s, p_r,
):
    KP, W, B = a_pat.shape[0], a_pat.shape[1], a_v.shape[1]
    NA, NJ = s_v.shape[1] // B, p_in.shape[0]
    waves = waves_of(KP, KEEP)
    NV, Q = len(waves), NJ // PARTS
    window = [WINDOW[min(v, len(WINDOW) - 1)] * R // 8 for v in range(NV)]
    Y = R // Z
    f32 = jnp.float32
    me, col = lax.axis_index("row"), lax.axis_index("col")
    z, y = lax.div(me, Y), lax.rem(me, Y)
    near0 = 2 * lax.div(z, 2)
    far0 = 2 - near0
    zn = 2 * near0 + 1 - z
    inner = (z == 1) | (z == 2)
    far_inner = jnp.where(z < 2, 2, 1)

    load_a = pltpu.make_async_copy(a_hbm, a_v.at[pl.ds(0, W * B * KP)], load.at[0])
    load_s = pltpu.make_async_copy(s_hbm, s_v, load.at[1])
    small = [
        pltpu.make_async_copy(src, dst, load.at[2 + i])
        for i, (src, dst) in enumerate(((owner_hbm, owner), (a_pat_hbm, a_pat), (p_pat_hbm, p_pat), (p_hbm, p_in)))
    ]
    load_a.start()
    for c in small:
        c.start()
    load_s.start()

    barrier = pltpu.get_barrier_semaphore()
    for i in range(1, R):
        pl.semaphore_signal(barrier, inc=1, device_id={"row": lax.rem(me + i, R)}, device_id_type=MESH)
    for i in range(1, C):
        pl.semaphore_signal(barrier, inc=1, device_id={"col": lax.rem(col + i, C)}, device_id_type=MESH)

    def pair(source, target):
        first, last = jnp.int32(W), jnp.int32(-1)
        for e in range(W):
            hit = lax.div(owner[source * W + e], W) == target
            first = jnp.minimum(first, jnp.where(hit, e, W))
            last = jnp.maximum(last, jnp.where(hit, e, -1))
        valid = last >= 0
        return (jnp.where(valid, first, 0), jnp.where(valid, last, 0)), valid

    def step_of(j):
        half = lax.div(j + 1, 2)
        return R // 2 + half * (1 - 2 * lax.rem(j, 2))

    def a_copy(v, step):
        at = pl.ds(0, min(waves[v][2], B - waves[v][1]))
        return pltpu.make_async_remote_copy(
            src_ref=asend.at[v, step, :, at], dst_ref=arecv.at[v, step, :, at],
            send_sem=a_s.at[v, step], recv_sem=a_r.at[v, step],
            device_id={"row": lax.rem(me + step, R)}, device_id_type=MESH,
        )

    def pack(buf, step, k):
        chosen, valid = pair(me, lax.rem(me + step, R))
        for s in range(CAP):
            scale = jnp.where(valid, a_pat[k, chosen[s]], 0).astype(f32)
            flip[s, 0:B, 0:B] = a_v[pl.ds(chosen[s] * (B * KP) + k, B, stride=KP), :] * scale
        for s in range(CAP):
            turned = flip[s].T
            for v, (block, first, rows) in enumerate(waves):
                if block == k:
                    buf[v, step, s, 0:rows] = turned[first : first + rows]

    def p_copy(slot, q, target, s_sem):
        at = pl.ds(q * Q, Q)
        return pltpu.make_async_remote_copy(
            src_ref=pbuf.at[slot, at, pl.ds(0, B)], dst_ref=pbuf.at[slot, at, pl.ds(0, B)], send_sem=s_sem, recv_sem=p_r.at[slot, q],
            device_id={"row": target}, device_id_type=MESH,
        )

    def p_near(q):
        return p_copy(me, q, zn * Y + y, pn_s.at[q])

    def p_far(q):
        return p_copy(me, q, far_inner * Y + y, pf_s.at[q])

    def p_forward(u, q):
        return p_copy((far0 + u) * Y + y, q, zn * Y + y, pw_s.at[u, q])

    def p_across(zo, i, q):
        return p_copy(zo * Y + y, q, z * Y + lax.rem(y + i, Y), py_s.at[zo, i, q])

    def p_arrived(slot, q):
        p_copy(slot, q, me, pn_s.at[q]).wait_recv()

    def all_across(zo, q):
        for i in range(1, Y):
            p_across(zo, i, q).start()

    def near_arrives(q):
        p_arrived(zn * Y + y, q)
        all_across(zn, q)

    def far_arrives(q):
        for u in range(2):
            p_arrived((far0 + u) * Y + y, q)

            @pl.when(inner)
            def _():
                p_forward(u, q).start()

            all_across(far0 + u, q)

    def tall(v):
        return pl.ds(0, waves[v][2])

    def mine(v):
        rows = waves[v][2]
        return pl.ds(pl.multiple_of(col * rows, rows), rows)

    def y_copy(v, i, h):
        target = lax.rem(y + i, Y)
        at = pl.ds(near0 if h else far0, 2)
        return pltpu.make_async_remote_copy(
            src_ref=macc.at[v, target, at, tall(v)], dst_ref=yrecv.at[v, i, at, tall(v)], send_sem=y_s.at[v, i, h], recv_sem=y_r.at[v, i, h],
            device_id={"row": z * Y + target}, device_id_type=MESH,
        )

    def f_copy(v):
        return pltpu.make_async_remote_copy(
            src_ref=nbuf.at[v, pl.ds(far0, 2), tall(v)], dst_ref=frecv.at[v, :, tall(v)], send_sem=f_s.at[v], recv_sem=f_r.at[v],
            device_id={"row": zn * Y + y}, device_id_type=MESH,
        )

    def n_copy(v):
        return pltpu.make_async_remote_copy(
            src_ref=nbuf.at[v, zn, tall(v)], dst_ref=nrecv.at[v, tall(v)], send_sem=n_s.at[v], recv_sem=n_r.at[v],
            device_id={"row": zn * Y + y}, device_id_type=MESH,
        )

    def c_copy(v, u):
        return pltpu.make_async_remote_copy(
            src_ref=nbuf.at[v, far0 + u, tall(v)], dst_ref=crecv.at[v, tall(v)], send_sem=c_s.at[v, u], recv_sem=c_r.at[v],
            device_id={"row": (far0 + u) * Y + y}, device_id_type=MESH,
        )

    def g_copy(v, i):
        at = mine(v)
        return pltpu.make_async_remote_copy(
            src_ref=mfull.at[v, at], dst_ref=mfull.at[v, at], send_sem=g_s.at[v, i], recv_sem=g_r.at[v, i],
            device_id={"col": lax.rem(col + i, C)}, device_id_type=MESH,
        )

    def over_y(v):
        for h in range(2):
            for i in range(1, Y):
                y_copy(v, i, h).start()

    def over_near(v):
        for h in range(2):
            at = pl.ds(near0 if h else far0, 2)
            acc = macc[v, y, at, tall(v)]
            for i in range(1, Y):
                y_copy(v, i, h).wait_recv()
                acc += yrecv[v, i, at, tall(v)]
            nbuf[v, at, tall(v)] = acc
            if h == 0:
                @pl.when(jnp.logical_not(inner))
                def _():
                    f_copy(v).start()
            else:
                n_copy(v).start()

    def over_middle(v):
        @pl.when(inner)
        def _():
            f_copy(v).wait_recv()
            nbuf[v, pl.ds(far0, 2), tall(v)] += frecv[v, :, tall(v)]
            for u in range(2):
                c_copy(v, u).start()

    def over_col(v):
        n_copy(v).wait_recv()
        c_copy(v, 0).wait_recv()
        mfull[v, mine(v)] = nbuf[v, z, tall(v)] + nrecv[v, tall(v)] + crecv[v, tall(v)]
        for i in range(1, C):
            g_copy(v, i).start()

    def m_copy(v, step):
        target = lax.rem(me + step, R)
        d = v - (NV - DIRECT)
        return pltpu.make_async_remote_copy(
            src_ref=macc.at[v, lax.rem(target, Y), lax.div(target, Y), tall(v)], dst_ref=mrecv.at[d, step, tall(v)],
            send_sem=m_s.at[d, step], recv_sem=m_r.at[d, step],
            device_id={"row": target}, device_id_type=MESH,
        )

    def over_rows(v):
        def one(j, carry):
            m_copy(v, step_of(j)).start()
            return carry

        lax.fori_loop(0, R - 1, one, 0)

    def col_after_rows(v):
        acc = macc[v, y, z, tall(v)]
        for step in range(1, R):
            m_copy(v, step).wait_recv()
            acc += mrecv[v - (NV - DIRECT), step, tall(v)]
        mfull[v, mine(v)] = acc
        for i in range(1, C):
            g_copy(v, i).start()

    def last_product(v):
        for i in range(1, C):
            g_copy(v, i).wait_recv()
        width = C * waves[v][2]
        for c in range(width // L):
            hi, lo = split(mfull[v, c * L : (c + 1) * L].T)
            mth[:, c * L : (c + 1) * L] = hi
            mtl[:, c * L : (c + 1) * L] = lo
        mh, ml, fh = mth[:, 0:width], mtl[:, 0:width], ph[v, 0:width]
        total[...] += dot(mh, fh) + (dot(mh, plo[v, 0:width]) + dot(ml, fh))

    flip[...] = jnp.zeros_like(flip)
    for v, (block, first, rows) in enumerate(waves):
        if first + rows > B:
            arecv[v, :, :, B - first : rows] = jnp.zeros((R, CAP, first + rows - B, L), f32)
    pbuf[:, :, B:L] = jnp.zeros((R, NJ, L - B, L), f32)
    for c in small:
        c.wait()
    load_a.wait()

    def first_pack(j, carry):
        pack(asend, step_of(j), 0)
        return carry

    lax.fori_loop(0, R - 1, first_pack, 0)
    pl.semaphore_wait(barrier, R + C - 2)

    def send(n):
        if n < NV * (R - 1):
            a_copy(n // (R - 1), step_of(jnp.int32(n % (R - 1)))).start()

    for n in range(window[0]):
        send(n)

    for k in range(1, KP):
        def later_pack(j, carry):
            pack(asend, step_of(j), k)
            return carry

        lax.fori_loop(0, R - 1, later_pack, 0)

    for n in range(NJ):
        pbuf[me, n] = jnp.zeros((L, L), f32)
        pbuf[me, n, 0:B, 0:B] = p_in[n, :, 0, :] * p_pat[0, n].astype(f32)
    for k in range(KP):
        pack(arecv, 0, k)
    stage[...] = jnp.zeros_like(stage)
    macc[...] = jnp.zeros_like(macc)
    total[...] = jnp.zeros_like(total)
    load_s.wait()

    def slab(step, keep):
        source = lax.rem(me - step + R, R)
        rows, valid = pair(source, me)
        for s in range(CAP):
            g = jnp.where(valid, owner[source * W + rows[s]] - me * W, 0)

            def one(b, carry):
                for h in range(2):
                    stage[2 * b + h, 0:B, 0:B] = s_v[g, pl.ds(2 * b + h, B, stride=NA), :]
                for h in range(2):
                    hi, lo = split(stage[2 * b + h])
                    sh[keep, b, s * L : (s + 1) * L, h * L : (h + 1) * L] = hi
                    sl[keep, b, s * L : (s + 1) * L, h * L : (h + 1) * L] = lo
                return carry

            lax.fori_loop(0, NA // 2, one, 0)

    def work(v, j, carry):
        rows = waves[v][2]
        step = jnp.where(j == 0, 0, step_of(j - 1))
        keep = step if KEEP else 0
        if v == 0 or not KEEP:
            slab(step, keep)

        @pl.when(j > 0)
        def _():
            a_copy(v, step).wait_recv()
            for other in range(v, NV):
                ahead = j - 1 + window[v] - (other - v) * (R - 1)

                @pl.when((ahead >= 0) & (ahead < R - 1))
                def _():
                    a_copy(other, step_of(ahead)).start()

        for s in range(CAP):
            hi, lo = split(arecv[v, step, s, tall(v)])
            ahl[0:rows, s * L : (s + 1) * L] = hi
            ahl[rows : 2 * rows, s * L : (s + 1) * L] = lo
        for b in range(NA // 2):
            both = dot(ahl[0 : 2 * rows], sh[keep, b])
            r = both[0:rows] + (both[rows : 2 * rows] + dot(ahl[0:rows], sl[keep, b]))
            for h in range(2):
                a = 2 * b + h
                macc[v, a % Y, a // Y, tall(v)] += r[:, h * L : (h + 1) * L]

        @pl.when(j == R - 1)
        def _():
            (over_y if v < NV - DIRECT else over_rows)(v)

        for when, act in todo:
            if when // R == v:
                pl.when(j == when % R)(act)
        return carry

    def own_starts():
        for q in range(PARTS):
            p_near(q).start()
            all_across(z, q)

    def near_comes():
        for q in range(PARTS):
            near_arrives(q)

    ends = []
    for v, (_, _, rows) in enumerate(waves):
        start = ends[-1] if ends else 0.0
        ends += [start + rows * (j + 1) / (R * KP * L) for j in range(R)]

    def place(when):
        for t, end in enumerate(ends):
            if when <= end:
                return t
        return NV * R + int((when - 1) * 1000)

    todo = [(place(OWN), own_starts), (place(NEAR), near_comes)]
    for q in range(PARTS):
        far = FAR[0] + (FAR[1] - FAR[0]) * q / max(PARTS - 1, 1)
        todo.append((place(far), lambda q=q: p_far(q).start()))
        todo.append((place(far + INTO), lambda q=q: pl.when(inner)(lambda: far_arrives(q))))
        todo.append((place(far + INTO + ONWARD), lambda q=q: pl.when(jnp.logical_not(inner))(lambda: far_arrives(q))))
    for v in range(NV - DIRECT):
        for d, act in enumerate((over_near, over_middle, over_col)):
            todo.append((place(ends[(v + 1) * R - 1] + SUMS[d]), lambda v=v, act=act: act(v)))
    for v in range(NV - DIRECT, NV):
        todo.append((max(place(LAST), NV * R), lambda v=v: col_after_rows(v)))
    todo.sort(key=lambda item: item[0])

    for v in range(NV):
        if v > 0:
            for n in range(window[v - 1], window[v]):
                send(v * (R - 1) + n)
        lax.fori_loop(0, R, functools.partial(work, v), 0)
    for when, act in todo:
        if when >= NV * R:
            act()

    for q in range(PARTS):
        for zo in range(Z):
            for i in range(1, Y):
                p_arrived(zo * Y + lax.rem(y + i, Y), q)

    def p_split(i, carry):
        c, n = lax.div(i, NJ), lax.rem(i, NJ)
        lanes = pl.ds(pl.multiple_of(n * L, L), L)
        for k in range(KP):
            hi, lo = split(pbuf[c * KP + k, n])
            for v, (block, first, rows) in enumerate(waves):
                if block == k:
                    at = pl.ds(pl.multiple_of(c * rows, rows), rows)
                    ph[v, at, lanes] = hi[first : first + rows]
                    plo[v, at, lanes] = lo[first : first + rows]
        return carry

    lax.fori_loop(0, C * NJ, p_split, 0)
    for v in range(NV):
        last_product(v)

    for n in range(NJ):
        out[0, n] = total[0:B, n * L : n * L + B]

    for v in range(NV):
        def sent(j, carry):
            a_copy(v, j + 1).wait_send()
            return carry

        lax.fori_loop(0, R - 1, sent, 0)
        if v < NV - DIRECT:
            for i in range(1, Y):
                for h in range(2):
                    y_copy(v, i, h).wait_send()
            n_copy(v).wait_send()

            @pl.when(inner)
            def _():
                for u in range(2):
                    c_copy(v, u).wait_send()

            @pl.when(jnp.logical_not(inner))
            def _():
                f_copy(v).wait_send()
        else:
            for step in range(1, R):
                m_copy(v, step).wait_send()
        for i in range(1, C):
            g_copy(v, i).wait_send()
    for q in range(PARTS):
        p_near(q).wait_send()
        p_far(q).wait_send()

        @pl.when(inner)
        def _():
            for u in range(2):
                p_forward(u, q).wait_send()

        for zo in range(Z):
            for i in range(1, Y):
                p_across(zo, i, q).wait_send()


def shards(a_blocks, a_pattern, row_owner, prolong, p_pattern, prolong_slab):
    R, C = lax.axis_size("row"), lax.axis_size("col")
    W, KP, B = a_blocks.shape[:3]
    NA, NJ = prolong_slab.shape[1], prolong.shape[1]
    f32, bf16 = jnp.float32, jnp.bfloat16
    keep = R * NA <= 64
    waves = waves_of(KP, keep)
    Y, NV, RV = R // Z, len(waves), max(rows for _, _, rows in waves)
    slots = R if keep else 1
    oper = a_blocks.transpose(0, 2, 1, 3).reshape(W * B * KP, B)
    slab = prolong_slab.transpose(0, 2, 1, 3).reshape(W, B * NA, B)
    dma = pltpu.SemaphoreType.DMA
    vmem = pl.BlockSpec(memory_space=pltpu.VMEM)
    hbm = pl.BlockSpec(memory_space=pl.ANY)
    return pl.pallas_call(
        functools.partial(kernel, R, C, keep),
        out_shape=jax.ShapeDtypeStruct((1, NJ, B, B), f32),
        in_specs=[hbm] * 6,
        out_specs=vmem,
        scratch_shapes=[
            pltpu.VMEM((W * B * KP + 8, B), f32),
            pltpu.VMEM((NJ, B, 1, B), f32),
            pltpu.SMEM(row_owner.shape, jnp.int32),
            pltpu.SMEM((KP, W), jnp.int32),
            pltpu.SMEM((1, NJ), jnp.int32),
            pltpu.VMEM((W, B * NA, B), f32),
            pltpu.VMEM((CAP, L, L), f32),
            pltpu.VMEM((NV, R, CAP, RV, L), f32),
            pltpu.VMEM((NV, R, CAP, RV, L), f32),
            pltpu.VMEM((NA, L, L), f32),
            pltpu.VMEM((slots, NA // 2, CAP * L, 2 * L), bf16),
            pltpu.VMEM((slots, NA // 2, CAP * L, 2 * L), bf16),
            pltpu.VMEM((2 * RV, CAP * L), bf16),
            pltpu.VMEM((NV, Y, Z, RV, L), f32),
            pltpu.VMEM((NV, Y, Z, RV, L), f32),
            pltpu.VMEM((NV, Z, RV, L), f32),
            pltpu.VMEM((NV, 2, RV, L), f32),
            pltpu.VMEM((NV, RV, L), f32),
            pltpu.VMEM((NV, RV, L), f32),
            pltpu.VMEM((max(DIRECT, 1), R, RV, L), f32),
            pltpu.VMEM((NV, C * RV, L), f32),
            pltpu.VMEM((L, C * RV), bf16),
            pltpu.VMEM((L, C * RV), bf16),
            pltpu.VMEM((R, NJ, L, L), f32),
            pltpu.VMEM((NV, C * RV, NJ * L), bf16),
            pltpu.VMEM((NV, C * RV, NJ * L), bf16),
            pltpu.VMEM((L, NJ * L), f32),
            dma((6,)),
            dma((NV, R)), dma((NV, R)),
            dma((NV, Y, 2)), dma((NV, Y, 2)),
            dma((NV,)), dma((NV,)), dma((NV,)), dma((NV,)),
            dma((NV, 2)), dma((NV,)),
            dma((max(DIRECT, 1), R)), dma((max(DIRECT, 1), R)),
            dma((NV, C)), dma((NV, C)),
            dma((PARTS,)), dma((PARTS,)), dma((2, PARTS)), dma((Z, Y, PARTS)), dma((R, PARTS)),
        ],
        compiler_params=pltpu.CompilerParams(
            collective_id=0, has_side_effects=True, vmem_limit_bytes=VMEM_LIMIT
        ),
    )(oper, slab, prolong.transpose(1, 2, 0, 3), row_owner, a_pattern.T, p_pattern)


def solution(mesh):
    in_specs = (
        P("row", "col", None, None),
        P("row", "col"),
        P(),
        P("row", "col", None, None),
        P("row", "col"),
        P("row", None, None, None),
    )
    out_specs = P("row", "col", None, None)
    return jax.shard_map(shards, mesh=mesh, in_specs=in_specs, out_specs=out_specs, check_vma=False)
```
